128 devices in a mesh: dp: 4 (over y), ctx: 8 (over z, x_hi), tensor: 4 (over x_lo, core).
Axes of the slice: x: 4 (x_hi: 2, x_lo: 2; x = x_hi * 2 + x_lo), y: 4, z: 4, core: 2. Of those that a mesh axis runs over, the one named last changes fastest.
Arguments:
- tokens: bfloat16 [4096, 4096], P(('dp', 'ctx')), may hold values from -6 to 6
- out_grad: bfloat16 [4096, 4096], P(('dp', 'ctx')), may hold values from -6 to 6
- expert_ids: int32 [4096, 8], P(('dp', 'ctx')), may hold values from 0 to 31, as said below
- gate_probs: float32 [4096, 8], P(('dp', 'ctx')), may hold values from 0.1 to 0.5
- w_gate: bfloat16 [32, 768, 4096], P(('ctx', 'tensor')), may hold values from -0.09375 to 0.09375
- w_up: bfloat16 [32, 768, 4096], P(('ctx', 'tensor')), may hold values from -0.09375 to 0.09375
- w_down: bfloat16 [32, 768, 4096], P(('ctx', 'tensor')), may hold values from -0.21875 to 0.21875
Outputs:
- in_grad: bfloat16 [4096, 4096], P(('dp', 'ctx', 'tensor'))
- grad_gate: bfloat16 [32, 768, 4096], P(('ctx', 'tensor'), 'dp')
- grad_up: bfloat16 [32, 768, 4096], P(('ctx', 'tensor'), 'dp')
- grad_down: bfloat16 [32, 768, 4096], P(('ctx', 'tensor'), 'dp')
The draws below stay inside these ranges and needn't reach their ends.
Inputs may be any that keep to these rules, and one draw needn't show every extreme that they name: `expert_ids`: each token names 8 different experts. Cut a token's slots into 4 runs of 2 consecutive slots; over the 128 tokens of one index pair of dp and ctx, one run names one expert at most 16 times, and in some run of every such block some expert exactly 16 times.
All inputs are finite; a program needn't handle non-finite values.
Results may differ from the reference program's by a relative error of at most 0.023.
Values may be sent and summed in bfloat16 or wider, within the bound.
No kernel may reach another device: no remote copies, remote signals or barrier semaphores. Data moves between devices by JAX's collectives and lax.ppermute only.
A program may use at most 192 MiB of HBM per device.

```python
import jax
import jax.numpy as jnp
from jax import lax

D = 4096
TOP = 8
FF = 768
T_DEV = 128
EXPERTS = 32
TOKENS = 4096
SLOTS = 2
SEND_CAP = 16
N_DP = 4
N_CTX = 8
N_TENSOR = 4


def draw_expert_ids(key, part):
    key = jax.random.fold_in(key, 7)
    block_count = TOKENS // T_DEV
    group_size = EXPERTS // 2
    group_count = T_DEV // group_size
    total_groups = block_count * group_count
    heavy_key, run_key, label_key, offset_key, score_key, shuffle_key = jax.random.split(key, 6)
    heavy_expert = jax.random.randint(heavy_key, (block_count,), 0, EXPERTS, dtype=jnp.int32)
    heavy_run = jax.random.randint(run_key, (block_count,), 0, N_TENSOR, dtype=jnp.int32)
    group_heavy = jnp.repeat(heavy_expert, group_count)
    group_run = jnp.repeat(heavy_run, group_count)
    labels = jax.vmap(lambda sub: jax.random.permutation(sub, EXPERTS))(jax.random.split(label_key, total_groups)).astype(jnp.int32)
    columns = jnp.arange(EXPERTS, dtype=jnp.int32)
    swapped = jnp.where(labels == group_heavy[:, None], labels[:, :1], labels)
    swapped = jnp.where(columns[None, :] == 0, group_heavy[:, None], swapped).astype(jnp.int32)
    offsets = jax.vmap(lambda sub: jax.random.permutation(sub, EXPERTS))(jax.random.split(offset_key, total_groups)).astype(jnp.int32)[:, :TOP]
    first_offset = jnp.take_along_axis(offsets, (group_run * SLOTS)[:, None], axis=1)
    second_offset = jnp.take_along_axis(offsets, (group_run * SLOTS + 1)[:, None], axis=1)
    forced = (columns[None, :] == -first_offset % EXPERTS) | (columns[None, :] == -second_offset % EXPERTS)
    ranks = jax.vmap(lambda sub: jax.random.permutation(sub, EXPERTS))(jax.random.split(score_key, total_groups)).astype(jnp.int32)
    scores = ranks + EXPERTS * jnp.where(forced, 0, 1).astype(jnp.int32)
    residues = jnp.argsort(scores, axis=1, stable=True)[:, :group_size].astype(jnp.int32)
    places = (residues[:, :, None] + offsets[:, None, :]) % EXPERTS
    values = jnp.take_along_axis(swapped, places.reshape(total_groups, group_size * TOP), axis=1)
    blocks = values.reshape(block_count, T_DEV, TOP)
    shuffled = jax.vmap(lambda sub, rows: jax.random.permutation(sub, rows, axis=0))(jax.random.split(shuffle_key, block_count), blocks)
    return shuffled.reshape(TOKENS, TOP).astype(jnp.int32)


def block_levels(stream_key, extent, shards, least, largest):
    level = 1.0
    for axis_at, parts in shards:
        steps = jax.random.uniform(jax.random.fold_in(jax.random.fold_in(stream_key, 6), axis_at), (parts,), jnp.float32, least / len(shards), largest / len(shards))
        level = level * jnp.repeat(jnp.exp(steps), extent[axis_at] // parts).reshape((-1,) + (1,) * (len(extent) - 1 - axis_at))
    return level


def scatter_about(key, shape, spread, reach, pieces=(), kind=jnp.bfloat16):
    drawn = jax.random.normal(key, shape, jnp.float32) * spread
    if len(pieces) > 0:
        drawn = block_levels(key, shape, pieces, -0.22, 0.18) * drawn
    return jnp.clip(drawn, min=-reach, max=reach).astype(kind)


def setup_inputs(seed: int = 0) -> dict:
    seeds = jax.random.split(jax.random.key(seed), 8)
    return {
        "tokens": scatter_about(seeds[0], (TOKENS, D), 1.0, 6.0, ((0, 32),)),
        "out_grad": scatter_about(seeds[1], (TOKENS, D), 1.0, 6.0, ((0, 32),)),
        "expert_ids": draw_expert_ids(jax.random.fold_in(seeds[7], 71), 0),
        "gate_probs": jnp.clip(0.1 + 0.4 * jax.random.uniform(seeds[3], (TOKENS, TOP), jnp.float32) ** block_levels(seeds[3], (TOKENS, TOP), ((0, 32),), -0.2, 0.2), 0.1, 0.5),
        "w_gate": scatter_about(seeds[4], (EXPERTS, FF, D), D ** -0.5, 0.09375, ((0, 32),)),
        "w_up": scatter_about(seeds[5], (EXPERTS, FF, D), D ** -0.5, 0.09375, ((0, 32),)),
        "w_down": scatter_about(seeds[6], (EXPERTS, FF, D), FF ** -0.5, 0.21875, ((0, 32),)),
    }


def silu_parts(gate_pre):
    sigmoid = jax.nn.sigmoid(gate_pre)
    return gate_pre * sigmoid, sigmoid * (1.0 + gate_pre * (1.0 - sigmoid))


def reference(tokens, out_grad, expert_ids, gate_probs, w_gate, w_up, w_down):
    group_tokens = tokens.shape[0] // N_DP
    model_width = tokens.shape[1]
    capacity = min(N_CTX * N_TENSOR * SEND_CAP, group_tokens)
    token_groups = tokens.reshape(N_DP, group_tokens, model_width)
    grad_groups = out_grad.reshape(N_DP, group_tokens, model_width)
    id_groups = expert_ids.reshape(N_DP, group_tokens, TOP)
    prob_groups = gate_probs.reshape(N_DP, group_tokens, TOP)
    pick_rows = jax.vmap(lambda table, index: table[index])

    def group_sum(hidden_side, feature_side):
        products = jnp.einsum("grf,grd->gfd", hidden_side.reshape(N_DP, capacity, -1).astype(jnp.float32), feature_side.reshape(N_DP, capacity, model_width).astype(jnp.float32))
        rounded = lax.optimization_barrier(products.astype(jnp.bfloat16))
        return jnp.sum(rounded.astype(jnp.float32), axis=0).astype(jnp.bfloat16)

    def one_expert(running, expert):
        hits = id_groups == expert
        chosen = jnp.any(hits, axis=2)
        weight = jnp.sum(jnp.where(hits, prob_groups, 0.0), axis=2)
        order = jnp.argsort(jnp.where(chosen, 0, 1).astype(jnp.int32), axis=1, stable=True)[:, :capacity].astype(jnp.int32)
        valid = pick_rows(chosen, order)
        probs = jnp.where(valid, pick_rows(weight, order), 0.0).reshape(-1)
        rows_in = jnp.where(valid[:, :, None], pick_rows(token_groups, order), 0.0).astype(jnp.bfloat16).reshape(-1, model_width)
        grads_in = jnp.where(valid[:, :, None], pick_rows(grad_groups, order), 0.0).astype(jnp.bfloat16).reshape(-1, model_width)
        gate_matrix = w_gate[expert]
        up_matrix = w_up[expert]
        down_matrix = w_down[expert]
        gate_pre = jnp.dot(rows_in, gate_matrix.T, preferred_element_type=jnp.float32)
        up_pre = jnp.dot(rows_in, up_matrix.T, preferred_element_type=jnp.float32)
        active, slope = silu_parts(gate_pre)
        scaled_hidden = (probs[:, None] * active * up_pre).astype(jnp.bfloat16)
        hidden_grad = probs[:, None] * jnp.dot(grads_in, down_matrix.T, preferred_element_type=jnp.float32)
        gate_rows = (hidden_grad * up_pre * slope).astype(jnp.bfloat16)
        up_rows = (hidden_grad * active).astype(jnp.bfloat16)
        input_rows = (jnp.dot(gate_rows, gate_matrix, preferred_element_type=jnp.float32) + jnp.dot(up_rows, up_matrix, preferred_element_type=jnp.float32)).astype(jnp.bfloat16)
        returned = jnp.where(valid[:, :, None], input_rows.reshape(N_DP, capacity, model_width).astype(jnp.float32), 0.0)
        running = jax.vmap(lambda acc, index, values: acc.at[index].add(values))(running, order, returned)
        return running, (group_sum(gate_rows, rows_in), group_sum(up_rows, rows_in), group_sum(scaled_hidden, grads_in))

    initial = jnp.zeros((N_DP, group_tokens, model_width), jnp.float32)
    summed, (grad_gate, grad_up, grad_down) = lax.scan(one_expert, initial, jnp.arange(w_gate.shape[0], dtype=jnp.int32))
    return summed.reshape(-1, model_width).astype(jnp.bfloat16), grad_gate, grad_up, grad_down
```

```python
import jax
import jax.numpy as jnp
from jax import lax
from jax.experimental import pallas as pl
from jax.experimental.pallas import tpu as pltpu
from jax.sharding import Mesh
from jax.sharding import PartitionSpec as P

BF16 = jnp.bfloat16
F32 = jnp.float32
VMEM_LIMIT = 56 * 1024 * 1024
PLANE = ("z", "xh", "xl", "core")
LANES = 128


def hidden_kernel(expert_ref, gathered_ref, gate_ref, up_ref, down_ref, out_ref, held, prob_ref, sems):
    unit, tile = pl.program_id(0), pl.program_id(1)
    rows = out_ref.shape[2]
    width = gate_ref.shape[1]

    def copy(index):
        span = pl.ds(pl.multiple_of(index * rows, rows), rows)
        return pltpu.make_async_copy(gathered_ref.at[span], held.at[span], sems.at[index])

    @pl.when((unit == 0) & (tile == 0))
    def _():
        for index in range(held.shape[0] // rows):
            copy(index).start()

    span = pl.ds(pl.multiple_of(tile * rows, rows), rows)

    @pl.when(unit == 0)
    def _():
        copy(tile).wait()
        lane = lax.broadcasted_iota(jnp.int32, (8, LANES), 1)
        expert = expert_ref[0]
        chosen = ((lane == expert) | (lane == expert + LANES // 2)).astype(F32).astype(BF16)
        prob_ref[:, span] = lax.dot_general(
            chosen, held[span, 2 * width :], (((1,), (1,)), ((), ())), preferred_element_type=F32
        )

    tokens = held[span, :width]
    grads = held[span, width : 2 * width]
    by_features = (((1,), (1,)), ((), ()))
    gate_pre = lax.dot_general(gate_ref[...], tokens, by_features, preferred_element_type=F32)
    up_pre = lax.dot_general(up_ref[...], tokens, by_features, preferred_element_type=F32)
    down_pre = lax.dot_general(down_ref[...], grads, by_features, preferred_element_type=F32)
    prob = prob_ref[0:1, span]
    sigmoid = jax.nn.sigmoid(gate_pre)
    active = gate_pre * sigmoid
    slope = sigmoid * (1.0 + gate_pre * (1.0 - sigmoid))
    hidden_grad = prob * down_pre
    out_ref[0] = (hidden_grad * up_pre * slope).astype(BF16)
    out_ref[1] = (hidden_grad * active).astype(BF16)
    out_ref[2] = (prob * active * up_pre).astype(BF16)


def hidden_rows(gathered, expert, w_gate, w_up, w_down):
    token_count = gathered.shape[0]
    units, width = w_gate.shape
    step, rows = 256, 256
    weight = pl.BlockSpec((step, width), lambda u, t, e: (u, 0))
    return pl.pallas_call(
        hidden_kernel,
        grid_spec=pltpu.PrefetchScalarGridSpec(
            num_scalar_prefetch=1,
            grid=(units // step, token_count // rows),
            in_specs=[pl.BlockSpec(memory_space=pl.ANY), weight, weight, weight],
            out_specs=pl.BlockSpec((3, step, rows), lambda u, t, e: (0, u, t)),
            scratch_shapes=[
                pltpu.VMEM(gathered.shape, BF16),
                pltpu.VMEM((8, token_count), F32),
                pltpu.SemaphoreType.DMA((token_count // rows,)),
            ],
        ),
        out_shape=jax.ShapeDtypeStruct((3, units, token_count), BF16),
        compiler_params=pltpu.CompilerParams(vmem_limit_bytes=VMEM_LIMIT),
        cost_estimate=pl.CostEstimate(
            flops=6 * token_count * units * width,
            bytes_accessed=2 * gathered.size + 6 * w_gate.size + 6 * token_count * units,
            transcendentals=token_count * units,
        ),
        name="hidden_rows",
    )(expert, gathered, w_gate, w_up, w_down)


def input_kernel(hidden_ref, gate_ref, up_ref, out_ref, turned):
    @pl.when(pl.program_id(0) == 0)
    def _():
        turned[0] = hidden_ref[0].T
        turned[1] = hidden_ref[1].T

    total = jnp.dot(turned[0], gate_ref[...], preferred_element_type=F32)
    total += jnp.dot(turned[1], up_ref[...], preferred_element_type=F32)
    total = total.astype(BF16).reshape(out_ref.shape[1], 2, out_ref.shape[2], out_ref.shape[3])
    out_ref[0] = total[:, 0]
    out_ref[1] = total[:, 1]


def input_rows(hidden, w_gate, w_up, share):
    _, units, token_count = hidden.shape
    width = w_gate.shape[1]
    step = 512
    groups = token_count // (2 * share)
    weight = pl.BlockSpec((units, step), lambda i: (0, i))
    return pl.pallas_call(
        input_kernel,
        grid=(width // step,),
        in_specs=[
            pl.BlockSpec((2, units, token_count), lambda i: (0, 0, 0)),
            weight,
            weight,
        ],
        out_specs=pl.BlockSpec((2, groups, share, step), lambda i: (0, 0, 0, i)),
        out_shape=jax.ShapeDtypeStruct((2, groups, share, width), BF16),
        scratch_shapes=[pltpu.VMEM((2, token_count, units), BF16)],
        compiler_params=pltpu.CompilerParams(vmem_limit_bytes=VMEM_LIMIT),
        cost_estimate=pl.CostEstimate(
            flops=4 * token_count * units * width,
            bytes_accessed=4 * w_gate.size + 2 * token_count * width,
            transcendentals=0,
        ),
        name="input_rows",
    )(hidden, w_gate, w_up)


def weight_kernel(hidden_ref, gathered_ref, out_ref):
    out_ref[0, 0] = jnp.dot(hidden_ref[0], gathered_ref[...], preferred_element_type=F32).astype(BF16)


def weight_grads(hidden, gathered, width, owners):
    _, units, token_count = hidden.shape
    share = units // owners
    return pl.pallas_call(
        weight_kernel,
        grid=(2, owners * 3),
        in_specs=[
            pl.BlockSpec((1, share, token_count), lambda h, i: (i % 3, i // 3, 0)),
            pl.BlockSpec((token_count, width // 2), lambda h, i: (0, h + 2 * ((i % 3) // 2))),
        ],
        out_specs=pl.BlockSpec((1, 1, share, width // 2), lambda h, i: (i // 3, i % 3, 0, h)),
        out_shape=jax.ShapeDtypeStruct((owners, 3, share, width), BF16),
        compiler_params=pltpu.CompilerParams(vmem_limit_bytes=VMEM_LIMIT),
        cost_estimate=pl.CostEstimate(
            flops=6 * token_count * units * width,
            bytes_accessed=4 * token_count * width + 6 * units * width,
            transcendentals=0,
        ),
        name="weight_grads",
    )(hidden, gathered)


def per_device(tokens, out_grad, expert_ids, gate_probs, w_gate, w_up, w_down):
    token_count, width = tokens.shape
    owners = lax.axis_size("dp")
    ranks = lax.axis_size(("xl", "core"))
    experts = lax.axis_size(PLANE)
    share = token_count // ranks
    rank = lax.axis_index(("xl", "core"))
    core = lax.axis_index("core")
    expert = lax.axis_index(PLANE)

    def own_share(array):
        return lax.dynamic_slice_in_dim(array, rank * share, share, 0)

    hits = own_share(expert_ids)[:, :, None] == jnp.arange(experts, dtype=jnp.int32)
    table = jnp.sum(jnp.where(hits, own_share(gate_probs)[:, :, None], 0.0), axis=1)
    coarse = table.astype(BF16)
    fine = (table - coarse.astype(F32)).astype(BF16)
    pad = jnp.zeros((share, LANES // 2 - experts), BF16)
    payload = jnp.concatenate(
        [own_share(tokens), own_share(out_grad), coarse, pad, fine, pad], axis=1
    )
    gathered = lax.all_gather(payload, PLANE, axis=0, tiled=True)
    hidden = hidden_rows(gathered, expert[None], w_gate[0], w_up[0], w_down[0])
    grads = weight_grads(hidden, gathered, width, owners)
    summed = lax.psum_scatter(
        grads.reshape(owners * 3, -1, width), "dp", scatter_dimension=0, tiled=True
    )
    hidden, grads = lax.optimization_barrier((hidden, grads))
    rows = input_rows(hidden, w_gate[0], w_up[0], share)
    kept = lax.dynamic_index_in_dim(rows, core, 0, keepdims=False)
    given = lax.dynamic_index_in_dim(rows, 1 - core, 0, keepdims=False)
    taken = lax.ppermute(given, "core", [(0, 1), (1, 0)])
    paired = (kept.astype(F32) + taken.astype(F32)).astype(BF16)
    returned = lax.all_to_all(paired, PLANE[:3], split_axis=0, concat_axis=0, tiled=True)
    in_grad = jnp.sum(returned.astype(F32), axis=0).astype(BF16)
    return (in_grad, summed[0:1], summed[1:2], summed[2:3])


def solution(mesh):
    dp, ctx, tensor = (mesh.shape[name] for name in ("dp", "ctx", "tensor"))
    fine = Mesh(
        mesh.devices.reshape(dp, ctx // 2, 2, tensor // 2, 2), ("dp", "z", "xh", "xl", "core")
    )
    token_spec = P(("dp", "z", "xh"), None)
    weight_spec = P(PLANE, None, None)
    grad_spec = P(PLANE, "dp", None)
    return jax.shard_map(
        per_device,
        mesh=fine,
        in_specs=(token_spec,) * 4 + (weight_spec,) * 3,
        out_specs=(P(("dp",) + PLANE, None), grad_spec, grad_spec, grad_spec),
        check_vma=False,
    )
```

```python
import jax
import jax.numpy as jnp
from jax import lax
from jax.experimental import pallas as pl
from jax.experimental.pallas import tpu as pltpu
from jax.sharding import Mesh
from jax.sharding import PartitionSpec as P

BF16 = jnp.bfloat16
F32 = jnp.float32
VMEM_LIMIT = 56 * 1024 * 1024
PLANE = ("z", "xh", "xl", "core")
LANES = 128


def hidden_kernel(
    route_ref, gathered_ref, gate_ref, up_ref, down_ref, out_ref, near_ref, far_ref,
    held, gate, up, down, token_sems, weight_sems,
):
    tile = pl.program_id(0)
    rows = out_ref.shape[3]
    share, width = gate_ref.shape[1], gate_ref.shape[2]
    weights = ((gate_ref, gate), (up_ref, up), (down_ref, down))

    def token_copy(index):
        span = pl.ds(pl.multiple_of(index * rows, rows), rows)
        return pltpu.make_async_copy(gathered_ref.at[span], held.at[index % 2], token_sems.at[index % 2])

    def weight_copy(which, place):
        source, target = weights[which]
        return pltpu.make_async_copy(
            source.at[route_ref[place]],
            target.at[pl.ds(place * share, share)],
            weight_sems.at[which, place],
        )

    @pl.when(tile == 0)
    def _():
        token_copy(0).start()
        for half in range(2):
            for which in range(3):
                for place in (2 * half, 2 * half + 1):
                    weight_copy(which, place).start()

    token_copy(tile).wait()

    @pl.when(tile + 1 < pl.num_programs(0))
    def _():
        token_copy(tile + 1).start()

    slot = tile % 2
    tokens = held[slot, :, :width]
    grads = held[slot, :, width : 2 * width]
    lane = lax.broadcasted_iota(jnp.int32, (8, LANES), 1)
    expert = route_ref[4]
    chosen = ((lane == expert) | (lane == expert + LANES // 2)).astype(F32).astype(BF16)
    by_features = (((1,), (1,)), ((), ()))
    prob = lax.dot_general(
        chosen, held[slot, :, 2 * width :], by_features, preferred_element_type=F32
    )[0:1]
    for half in range(2):
        span = pl.ds(2 * half * share, 2 * share)

        def product(which, array, right):
            @pl.when(tile == 0)
            def _():
                weight_copy(which, 2 * half).wait()
                weight_copy(which, 2 * half + 1).wait()

            return lax.dot_general(array[span], right, by_features, preferred_element_type=F32)

        gate_pre = product(0, gate, tokens)
        up_pre = product(1, up, tokens)
        hidden_grad = prob * product(2, down, grads)
        sigmoid = jax.nn.sigmoid(gate_pre)
        active = gate_pre * sigmoid
        slope = sigmoid * (1.0 + gate_pre * (1.0 - sigmoid))
        results = (hidden_grad * up_pre * slope, hidden_grad * active, prob * active * up_pre)
        for which, result in enumerate(results):
            result = result.astype(BF16).reshape(2, share, rows)
            out_ref[which, route_ref[2 * half]] = result[0]
            out_ref[which, route_ref[2 * half + 1]] = result[1]
            if half == 0:
                near_ref[which] = result
                far_ref[which, 0] = result[1]
            else:
                far_ref[which, 1] = result[0]


def hidden_rows(gathered, route, w_gate, w_up, w_down):
    token_count = gathered.shape[0]
    owners, share, width = w_gate.shape
    rows = 256
    whole = pl.BlockSpec(memory_space=pl.ANY)
    kept = pltpu.VMEM((owners * share, width), BF16)
    pair = pl.BlockSpec((3, 2, share, rows), lambda t, r: (0, 0, 0, t))
    return pl.pallas_call(
        hidden_kernel,
        grid_spec=pltpu.PrefetchScalarGridSpec(
            num_scalar_prefetch=1,
            grid=(token_count // rows,),
            in_specs=[whole, whole, whole, whole],
            out_specs=[pl.BlockSpec((3, owners, share, rows), lambda t, r: (0, 0, 0, t)), pair, pair],
            scratch_shapes=[
                pltpu.VMEM((2, rows, gathered.shape[1]), BF16),
                kept,
                kept,
                kept,
                pltpu.SemaphoreType.DMA((2,)),
                pltpu.SemaphoreType.DMA((3, owners)),
            ],
        ),
        out_shape=[
            jax.ShapeDtypeStruct((3, owners, share, token_count), BF16),
            jax.ShapeDtypeStruct((3, 2, share, token_count), BF16),
            jax.ShapeDtypeStruct((3, 2, share, token_count), BF16),
        ],
        compiler_params=pltpu.CompilerParams(vmem_limit_bytes=VMEM_LIMIT),
        cost_estimate=pl.CostEstimate(
            flops=6 * token_count * w_gate.size,
            bytes_accessed=2 * gathered.size + 6 * w_gate.size,
            transcendentals=token_count * owners * share,
        ),
        name="hidden_rows",
    )(route, gathered, w_gate, w_up, w_down)


def input_kernel(hidden_ref, gate_ref, up_ref, out_ref, turned):
    @pl.when(pl.program_id(0) == 0)
    def _():
        turned[0] = hidden_ref[0].T
        turned[1] = hidden_ref[1].T

    total = jnp.dot(turned[0], gate_ref[...], preferred_element_type=F32)
    total += jnp.dot(turned[1], up_ref[...], preferred_element_type=F32)
    total = total.astype(BF16).reshape(out_ref.shape[1], 2, out_ref.shape[2], out_ref.shape[3])
    out_ref[0] = total[:, 0]
    out_ref[1] = total[:, 1]


def input_rows(hidden, w_gate, w_up, share):
    _, units, token_count = hidden.shape
    width = w_gate.shape[1]
    step = 512
    groups = token_count // (2 * share)
    weight = pl.BlockSpec((units, step), lambda i: (0, i))
    return pl.pallas_call(
        input_kernel,
        grid=(width // step,),
        in_specs=[
            pl.BlockSpec((2, units, token_count), lambda i: (0, 0, 0)),
            weight,
            weight,
        ],
        out_specs=pl.BlockSpec((2, groups, share, step), lambda i: (0, 0, 0, i)),
        out_shape=jax.ShapeDtypeStruct((2, groups, share, width), BF16),
        scratch_shapes=[pltpu.VMEM((2, token_count, units), BF16)],
        compiler_params=pltpu.CompilerParams(vmem_limit_bytes=VMEM_LIMIT),
        cost_estimate=pl.CostEstimate(
            flops=4 * token_count * units * width,
            bytes_accessed=4 * w_gate.size + 2 * token_count * width,
            transcendentals=0,
        ),
        name="input_rows",
    )(hidden, w_gate, w_up)


def weight_kernel(
    pick_ref, first_ref, second_ref, other_ref, own_ref, near_ref, out_first, out_second, left
):
    share = first_ref.shape[2]

    @pl.when(pl.program_id(0) == 0)
    def _():
        left[0, :share] = first_ref[0, 0]
        left[0, share:] = second_ref[0, 0]
        left[1, :share] = other_ref[0, 0]
        left[1, share:] = other_ref[0, 1]

    total = jnp.dot(left[0], own_ref[...], preferred_element_type=F32)
    total += jnp.dot(left[1], near_ref[...], preferred_element_type=F32)
    out_first[...] = total[:share].astype(BF16)
    out_second[...] = total[share:].astype(BF16)


def weight_grads(which, half, picks, hidden, other, gathered, gathered_near):
    _, _, share, token_count = hidden.shape
    width = gathered_near.shape[1] // 2
    columns = width // 2
    step = 512
    count = columns // step
    own_base = ((which // 2) * 2 + half) * count
    near_base = (half * 2 + which // 2) * count
    out = pl.BlockSpec((share, step), lambda i, p: (0, i))
    shape = jax.ShapeDtypeStruct((share, columns), BF16)
    return pl.pallas_call(
        weight_kernel,
        grid_spec=pltpu.PrefetchScalarGridSpec(
            num_scalar_prefetch=1,
            grid=(count,),
            in_specs=[
                pl.BlockSpec((1, 1, share, token_count), lambda i, p: (which, p[0], 0, 0)),
                pl.BlockSpec((1, 1, share, token_count), lambda i, p: (which, p[1], 0, 0)),
                pl.BlockSpec((1, 2, share, token_count), lambda i, p: (which, 0, 0, 0)),
                pl.BlockSpec((token_count, step), lambda i, p: (0, own_base + i)),
                pl.BlockSpec((token_count, step), lambda i, p: (0, near_base + i)),
            ],
            out_specs=[out, out],
            scratch_shapes=[pltpu.VMEM((2, 2 * share, token_count), BF16)],
        ),
        out_shape=[shape, shape],
        compiler_params=pltpu.CompilerParams(vmem_limit_bytes=VMEM_LIMIT),
        cost_estimate=pl.CostEstimate(
            flops=8 * share * token_count * columns,
            bytes_accessed=4 * token_count * columns + 12 * share * token_count,
            transcendentals=0,
        ),
        name="weight_grads",
    )(picks, hidden, hidden, other, gathered, gathered_near)


def per_device(tokens, out_grad, expert_ids, gate_probs, w_gate, w_up, w_down):
    token_count, width = tokens.shape
    half = width // 2
    owners = lax.axis_size("dp")
    ranks = lax.axis_size(("xl", "core"))
    experts = lax.axis_size(PLANE)
    units = w_gate.shape[1]
    share = token_count // ranks
    rank = lax.axis_index(("xl", "core"))
    core = lax.axis_index("core")
    expert = lax.axis_index(PLANE)
    place = lax.axis_index("dp")
    side = place ^ 1
    mirror = owners - 1 - place
    to_side = [(i, i ^ 1) for i in range(owners)]
    to_mirror = [(i, owners - 1 - i) for i in range(owners)]

    def own_share(array):
        return lax.dynamic_slice_in_dim(array, rank * share, share, 0)

    my_tokens, my_grads = own_share(tokens), own_share(out_grad)
    hits = own_share(expert_ids)[:, :, None] == jnp.arange(experts, dtype=jnp.int32)
    table = jnp.sum(jnp.where(hits, own_share(gate_probs)[:, :, None], 0.0), axis=1)
    coarse = table.astype(BF16)
    fine = (table - coarse.astype(F32)).astype(BF16)
    pad = jnp.zeros((share, LANES // 2 - experts), BF16)
    payload = jnp.concatenate([my_tokens, my_grads, coarse, pad, fine, pad], axis=1)
    gathered = lax.all_gather(payload, PLANE, axis=0, tiled=True)
    from_side = lax.ppermute(
        jnp.concatenate([my_tokens[:, :half], my_grads[:, :half]], axis=1), "dp", to_side
    )
    from_mirror = lax.ppermute(
        jnp.concatenate([my_tokens[:, half:], my_grads[:, half:]], axis=1), "dp", to_mirror
    )
    near_payload = jnp.concatenate([from_side, from_mirror], axis=1)
    gathered, near_payload = lax.optimization_barrier((gathered, near_payload))
    gathered_near = lax.all_gather(near_payload, PLANE, axis=0, tiled=True)

    route = jnp.stack([side, place ^ 2, mirror, place, expert]).astype(jnp.int32)
    gate, up, down = (w.reshape(owners, units // owners, width) for w in (w_gate, w_up, w_down))
    hidden, for_side, for_mirror = hidden_rows(gathered, route, gate, up, down)
    other_side = lax.ppermute(for_side, "dp", to_side)
    other_mirror = lax.ppermute(for_mirror, "dp", to_mirror)

    rows = input_rows(hidden.reshape(3, units, -1), w_gate[0], w_up[0], share)
    kept = lax.dynamic_index_in_dim(rows, core, 0, keepdims=False)
    given = lax.dynamic_index_in_dim(rows, 1 - core, 0, keepdims=False)
    taken = lax.ppermute(given, "core", [(0, 1), (1, 0)])
    paired = (kept.astype(F32) + taken.astype(F32)).astype(BF16)
    returned = lax.all_to_all(paired, PLANE[:3], split_axis=0, concat_axis=0, tiled=True)
    in_grad = jnp.sum(returned.astype(F32), axis=0).astype(BF16)

    low_picks = jnp.stack([place, mirror]).astype(jnp.int32)
    high_picks = jnp.stack([side, place]).astype(jnp.int32)
    results = []
    for which in range(3):
        mine_low, theirs_low = weight_grads(
            which, 0, low_picks, hidden, other_side, gathered, gathered_near
        )
        low = lax.ppermute(theirs_low, "dp", to_mirror)
        theirs_high, mine_high = weight_grads(
            which, 1, high_picks, hidden, other_mirror, gathered, gathered_near
        )
        high = lax.ppermute(theirs_high, "dp", to_side)
        low = mine_low.astype(F32) + low.astype(F32)
        high = mine_high.astype(F32) + high.astype(F32)
        results.append(jnp.concatenate([low, high], axis=1).astype(BF16)[None])
    return (in_grad, *results)


def solution(mesh):
    dp, ctx, tensor = (mesh.shape[name] for name in ("dp", "ctx", "tensor"))
    fine = Mesh(
        mesh.devices.reshape(dp, ctx // 2, 2, tensor // 2, 2), ("dp", "z", "xh", "xl", "core")
    )
    token_spec = P(("dp", "z", "xh"), None)
    weight_spec = P(PLANE, None, None)
    grad_spec = P(PLANE, "dp", None)
    return jax.shard_map(
        per_device,
        mesh=fine,
        in_specs=(token_spec,) * 4 + (weight_spec,) * 3,
        out_specs=(P(("dp",) + PLANE, None), grad_spec, grad_spec, grad_spec),
        check_vma=False,
    )
```

```python
import functools

import jax
import jax.numpy as jnp
from jax import lax
from jax.experimental import pallas as pl
from jax.experimental.pallas import tpu as pltpu
from jax.sharding import Mesh
from jax.sharding import PartitionSpec as P

BF16 = jnp.bfloat16
F32 = jnp.float32
VMEM_LIMIT = 56 * 1024 * 1024
PLANE = ("z", "xh", "xl", "core")
LANES = 128
SMALL = pl.CostEstimate(flops=0, bytes_accessed=0, transcendentals=0)


def hidden_kernel(
    start, route_ref, gathered_ref, gate_ref, up_ref, down_ref, out_ref, near_ref, far_ref,
    held, gate, up, down, token_sems, weight_sems,
):
    rows = out_ref.shape[3]
    owners, share, width = gate_ref.shape
    block = 256
    weights = ((gate_ref, gate), (up_ref, up), (down_ref, down))

    def token_copy(part):
        columns = pl.ds(0, width) if part == 0 else pl.ds(width, held.shape[1] - width)
        return pltpu.make_async_copy(
            gathered_ref.at[pl.ds(start, rows), columns], held.at[:, columns], token_sems.at[part]
        )

    def weight_copy(which, place):
        source, target = weights[which]
        return pltpu.make_async_copy(
            source.at[route_ref[place]],
            target.at[pl.ds(place * share, share)],
            weight_sems.at[which, place],
        )

    token_copy(0).start()
    for which in range(3):
        if which == 2:
            token_copy(1).start()
        weight_copy(which, 0).start()
        weight_copy(which, 1).start()
    for place in range(2, owners):
        for which in range(3):
            weight_copy(which, place).start()

    by_features = (((1,), (1,)), ((), ()))
    pieces = ([], [], [])
    for third in range(3):
        span = pl.ds(third * block, block)

        def wait(which):
            if third == 0:
                weight_copy(which, 0).wait()
                weight_copy(which, 1).wait()
            else:
                weight_copy(which, third + 1).wait()

        def product(array, right):
            return lax.dot_general(array[span], right, by_features, preferred_element_type=F32)

        if third == 0:
            token_copy(0).wait()
        wait(0)
        gate_pre = product(gate, held[:, :width])
        wait(1)
        up_pre = product(up, held[:, :width])
        if third == 0:
            token_copy(1).wait()
            lane = lax.broadcasted_iota(jnp.int32, (8, LANES), 1)
            expert = route_ref[4]
            chosen = ((lane == expert) | (lane == expert + LANES // 2)).astype(F32).astype(BF16)
            prob = lax.dot_general(
                chosen, held[:, 2 * width :], by_features, preferred_element_type=F32
            )[0:1]
        wait(2)
        hidden_grad = prob * product(down, held[:, width : 2 * width])
        sigmoid = jax.nn.sigmoid(gate_pre)
        active = gate_pre * sigmoid
        slope = sigmoid * (1.0 + gate_pre * (1.0 - sigmoid))
        pieces[0].append((hidden_grad * up_pre * slope).astype(BF16))
        pieces[1].append((hidden_grad * active).astype(BF16))
        pieces[2].append((prob * active * up_pre).astype(BF16))
    for which in range(3):
        result = jnp.concatenate(pieces[which], axis=0).reshape(owners, share, rows)
        for place in range(owners):
            out_ref[which, route_ref[place]] = result[place]
        near_ref[which] = result[0:2]
        far_ref[which] = result[1:3]


def hidden_rows(gathered, start, rows, route, w_gate, w_up, w_down):
    owners, share, width = w_gate.shape
    whole = pl.BlockSpec(memory_space=pl.ANY)
    kept = pltpu.VMEM((owners * share, width), BF16)
    pair = pl.BlockSpec((3, 2, share, rows), lambda t, r: (0, 0, 0, 0))
    return pl.pallas_call(
        functools.partial(hidden_kernel, start),
        grid_spec=pltpu.PrefetchScalarGridSpec(
            num_scalar_prefetch=1,
            grid=(1,),
            in_specs=[whole, whole, whole, whole],
            out_specs=[pl.BlockSpec((3, owners, share, rows), lambda t, r: (0, 0, 0, 0)), pair, pair],
            scratch_shapes=[
                pltpu.VMEM((rows, gathered.shape[1]), BF16),
                kept,
                kept,
                kept,
                pltpu.SemaphoreType.DMA((2,)),
                pltpu.SemaphoreType.DMA((3, owners)),
            ],
        ),
        out_shape=[
            jax.ShapeDtypeStruct((3, owners, share, rows), BF16),
            jax.ShapeDtypeStruct((3, 2, share, rows), BF16),
            jax.ShapeDtypeStruct((3, 2, share, rows), BF16),
        ],
        compiler_params=pltpu.CompilerParams(vmem_limit_bytes=VMEM_LIMIT),
        cost_estimate=SMALL,
        name="hidden_rows",
    )(route, gathered, w_gate, w_up, w_down)


def input_kernel(core_ref, hidden_ref, gate_ref, up_ref, kept_ref, given_ref, turned):
    @pl.when(pl.program_id(0) == 0)
    def _():
        turned[0] = hidden_ref[0].T
        turned[1] = hidden_ref[1].T

    total = jnp.dot(turned[0], gate_ref[...], preferred_element_type=F32)
    total += jnp.dot(turned[1], up_ref[...], preferred_element_type=F32)
    groups, share, step = kept_ref.shape
    total = total.astype(BF16).reshape(groups, 2, share, step)

    @pl.when(core_ref[0] == 0)
    def _():
        kept_ref[...] = total[:, 0]
        given_ref[...] = total[:, 1]

    @pl.when(core_ref[0] != 0)
    def _():
        kept_ref[...] = total[:, 1]
        given_ref[...] = total[:, 0]


def input_rows(hidden, core, w_gate, w_up, share):
    _, units, token_count = hidden.shape
    width = w_gate.shape[1]
    step = 512
    groups = token_count // (2 * share)
    weight = pl.BlockSpec((units, step), lambda i, c: (0, i))
    part = pl.BlockSpec((groups, share, step), lambda i, c: (0, 0, i))
    shape = jax.ShapeDtypeStruct((groups, share, width), BF16)
    return pl.pallas_call(
        input_kernel,
        grid_spec=pltpu.PrefetchScalarGridSpec(
            num_scalar_prefetch=1,
            grid=(width // step,),
            in_specs=[pl.BlockSpec((2, units, token_count), lambda i, c: (0, 0, 0)), weight, weight],
            out_specs=[part, part],
            scratch_shapes=[pltpu.VMEM((2, token_count, units), BF16)],
        ),
        out_shape=[shape, shape],
        compiler_params=pltpu.CompilerParams(vmem_limit_bytes=VMEM_LIMIT),
        cost_estimate=SMALL,
        name="input_rows",
    )(core, hidden, w_gate, w_up)


def own_kernel(
    pick_ref, first_ref, second_ref, tokens_ref, grads_ref, gate_ref, up_ref, down_ref, left
):
    share = first_ref.shape[2]

    @pl.when(pl.program_id(1) == 0)
    def _():
        for which in range(3):
            left[2 * share * which : 2 * share * which + share] = first_ref[which, 0]
            left[2 * share * which + share : 2 * share * (which + 1)] = second_ref[which, 0]

    both = jnp.dot(left[: 4 * share], tokens_ref[...], preferred_element_type=F32)
    gate_ref[0] = both[: 2 * share]
    up_ref[0] = both[2 * share :]
    down_ref[0] = jnp.dot(left[4 * share :], grads_ref[...], preferred_element_type=F32)


def own_grads(picks, hidden, gathered, width):
    _, _, share, token_count = hidden.shape
    step = 512
    count = width // 2 // step
    out = pl.BlockSpec((1, 2 * share, step), lambda h, i, p: (h, 0, i))
    shape = jax.ShapeDtypeStruct((2, 2 * share, width // 2), F32)
    return pl.pallas_call(
        own_kernel,
        grid_spec=pltpu.PrefetchScalarGridSpec(
            num_scalar_prefetch=1,
            grid=(2, count),
            in_specs=[
                pl.BlockSpec((3, 1, share, token_count), lambda h, i, p: (0, p[2 * h], 0, 0)),
                pl.BlockSpec((3, 1, share, token_count), lambda h, i, p: (0, p[2 * h + 1], 0, 0)),
                pl.BlockSpec((token_count, step), lambda h, i, p: (0, h * count + i)),
                pl.BlockSpec((token_count, step), lambda h, i, p: (0, (2 + h) * count + i)),
            ],
            out_specs=[out, out, out],
            scratch_shapes=[pltpu.VMEM((6 * share, token_count), BF16)],
        ),
        out_shape=[shape, shape, shape],
        compiler_params=pltpu.CompilerParams(vmem_limit_bytes=VMEM_LIMIT),
        cost_estimate=SMALL,
        name="own_grads",
    )(picks, hidden, hidden, gathered, gathered)


def weight_kernel(other_ref, near_ref, own_ref, out_first, out_second):
    share = out_first.shape[0]
    left = other_ref[0].reshape(2 * share, other_ref.shape[3])
    total = own_ref[0] + jnp.dot(left, near_ref[...], preferred_element_type=F32)
    out_first[...] = total[:share].astype(BF16)
    out_second[...] = total[share:].astype(BF16)


def weight_grads(which, half, other, gathered_near, own):
    _, _, share, token_count = other.shape
    columns = gathered_near.shape[1] // 4
    step = 512
    count = columns // step
    near_base = (half * 2 + which // 2) * count
    out = pl.BlockSpec((share, step), lambda i: (0, i))
    shape = jax.ShapeDtypeStruct((share, columns), BF16)
    return pl.pallas_call(
        weight_kernel,
        grid=(count,),
        in_specs=[
            pl.BlockSpec((1, 2, share, token_count), lambda i: (which, 0, 0, 0)),
            pl.BlockSpec((token_count, step), lambda i: (0, near_base + i)),
            pl.BlockSpec((1, 2 * share, step), lambda i: (half, 0, i)),
        ],
        out_specs=[out, out],
        out_shape=[shape, shape],
        compiler_params=pltpu.CompilerParams(vmem_limit_bytes=VMEM_LIMIT),
        cost_estimate=SMALL,
        name="weight_grads",
    )(other, gathered_near, own)


def per_device(tokens, out_grad, expert_ids, gate_probs, w_gate, w_up, w_down):
    token_count, width = tokens.shape
    half = width // 2
    owners = lax.axis_size("dp")
    ranks = lax.axis_size(("xl", "core"))
    experts = lax.axis_size(PLANE)
    units = w_gate.shape[1]
    share = token_count // ranks
    rank = lax.axis_index(("xl", "core"))
    core = lax.axis_index("core")
    expert = lax.axis_index(PLANE)
    place = lax.axis_index("dp")
    side = place ^ 1
    mirror = owners - 1 - place
    to_side = [(i, i ^ 1) for i in range(owners)]
    to_mirror = [(i, owners - 1 - i) for i in range(owners)]

    def own_share(array):
        return lax.dynamic_slice_in_dim(array, rank * share, share, 0)

    my_tokens, my_grads = own_share(tokens), own_share(out_grad)
    hits = own_share(expert_ids)[:, :, None] == jnp.arange(experts, dtype=jnp.int32)
    table = jnp.sum(jnp.where(hits, own_share(gate_probs)[:, :, None], 0.0), axis=1)
    coarse = table.astype(BF16)
    fine = (table - coarse.astype(F32)).astype(BF16)
    pad = jnp.zeros((share, LANES // 2 - experts), BF16)
    payload = jnp.concatenate([my_tokens, my_grads, coarse, pad, fine, pad], axis=1)
    gathered = lax.all_gather(payload, PLANE, axis=0, tiled=True)
    from_side = lax.ppermute(
        jnp.concatenate([my_tokens[:, :half], my_grads[:, :half]], axis=1), "dp", to_side
    )
    from_mirror = lax.ppermute(
        jnp.concatenate([my_tokens[:, half:], my_grads[:, half:]], axis=1), "dp", to_mirror
    )
    near_payload = jnp.concatenate([from_side, from_mirror], axis=1)
    gathered, near_payload = lax.optimization_barrier((gathered, near_payload))
    gathered_near = lax.all_gather(near_payload, PLANE, axis=0, tiled=True)

    route = jnp.stack([side, place ^ 2, mirror, place, expert]).astype(jnp.int32)
    gate, up, down = (w.reshape(owners, units // owners, width) for w in (w_gate, w_up, w_down))
    hidden, for_side, for_mirror = hidden_rows(
        gathered, 0, gathered.shape[0], route, gate, up, down
    )
    other_side = lax.ppermute(for_side, "dp", to_side)
    other_mirror = lax.ppermute(for_mirror, "dp", to_mirror)

    kept, given = input_rows(
        hidden.reshape(3, units, -1), core[None], w_gate[0], w_up[0], share
    )
    picks = jnp.stack([place, mirror, side, place]).astype(jnp.int32)
    own = own_grads(picks, hidden, gathered, width)
    kept, given, own, other_side, other_mirror = lax.optimization_barrier(
        (kept, given, own, other_side, other_mirror)
    )
    taken = lax.ppermute(given, "core", [(0, 1), (1, 0)])
    paired = (kept.astype(F32) + taken.astype(F32)).astype(BF16)
    returned = lax.all_to_all(paired, PLANE[:3], split_axis=0, concat_axis=0, tiled=True)

    mine, theirs = [], []
    for which in (2, 0, 1):
        mine_low, theirs_low = weight_grads(which, 0, other_side, gathered_near, own[which])
        theirs_high, mine_high = weight_grads(which, 1, other_mirror, gathered_near, own[which])
        mine.append((mine_low, mine_high))
        theirs.append((theirs_low, theirs_high))
    results = []
    for (mine_low, mine_high), (theirs_low, theirs_high) in zip(mine, theirs):
        low = mine_low.astype(F32) + lax.ppermute(theirs_low, "dp", to_mirror).astype(F32)
        high = mine_high.astype(F32) + lax.ppermute(theirs_high, "dp", to_side).astype(F32)
        results.append(jnp.concatenate([low, high], axis=1).astype(BF16)[None])
    returned, results = lax.optimization_barrier((returned, results))
    in_grad = jnp.sum(returned.astype(F32), axis=0).astype(BF16)
    return (in_grad, results[1], results[2], results[0])


def solution(mesh):
    dp, ctx, tensor = (mesh.shape[name] for name in ("dp", "ctx", "tensor"))
    fine = Mesh(
        mesh.devices.reshape(dp, ctx // 2, 2, tensor // 2, 2), ("dp", "z", "xh", "xl", "core")
    )
    token_spec = P(("dp", "z", "xh"), None)
    weight_spec = P(PLANE, None, None)
    grad_spec = P(PLANE, "dp", None)
    return jax.shard_map(
        per_device,
        mesh=fine,
        in_specs=(token_spec,) * 4 + (weight_spec,) * 3,
        out_specs=(P(("dp",) + PLANE, None), grad_spec, grad_spec, grad_spec),
        check_vma=False,
    )
```

```python
import functools

import jax
import jax.numpy as jnp
from jax import lax
from jax.experimental import pallas as pl
from jax.experimental.pallas import tpu as pltpu
from jax.sharding import Mesh
from jax.sharding import PartitionSpec as P

BF16 = jnp.bfloat16
F32 = jnp.float32
VMEM_LIMIT = 56 * 1024 * 1024
PLANE = ("z", "xh", "xl", "core")
LANES = 128
GIVEN = 4
SMALL = pl.CostEstimate(flops=0, bytes_accessed=0, transcendentals=0)


def hidden_kernel(
    start, route_ref, gathered_ref, gate_ref, up_ref, down_ref, out_ref, near_ref, far_ref,
    held, gate, up, down, stage, token_sems, weight_sems, out_sems,
):
    rows = stage.shape[2]
    owners, share, width = gate_ref.shape
    block = 256
    weights = ((gate_ref, gate), (up_ref, up), (down_ref, down))

    def token_copy(part):
        columns = pl.ds(0, width) if part == 0 else pl.ds(width, held.shape[1] - width)
        return pltpu.make_async_copy(
            gathered_ref.at[pl.ds(start, rows), columns], held.at[:, columns], token_sems.at[part]
        )

    def weight_copy(which, place):
        source, target = weights[which]
        return pltpu.make_async_copy(
            source.at[route_ref[place]],
            target.at[pl.ds(place * share, share)],
            weight_sems.at[which, place],
        )

    token_copy(0).start()
    for which in range(3):
        if which == 2:
            token_copy(1).start()
        weight_copy(which, 0).start()
        weight_copy(which, 1).start()
    for place in range(2, owners):
        for which in range(3):
            weight_copy(which, place).start()

    def flush(place):
        source = stage.at[:, pl.ds(place * share, share)]
        targets = [out_ref.at[:, route_ref[place]]]
        if place < 2:
            targets.append(near_ref.at[:, place])
        if 0 < place < 3:
            targets.append(far_ref.at[:, place - 1])
        return [
            pltpu.make_async_copy(source, target, out_sems.at[place, index])
            for index, target in enumerate(targets)
        ]

    by_features = (((1,), (1,)), ((), ()))
    for third in range(3):
        span = pl.ds(third * block, block)

        def wait(which):
            if third == 0:
                weight_copy(which, 0).wait()
                weight_copy(which, 1).wait()
            else:
                weight_copy(which, third + 1).wait()

        def product(array, right):
            return lax.dot_general(array[span], right, by_features, preferred_element_type=F32)

        if third == 0:
            token_copy(0).wait()
        wait(0)
        gate_pre = product(gate, held[:, :width])
        wait(1)
        up_pre = product(up, held[:, :width])
        if third == 0:
            token_copy(1).wait()
            lane = lax.broadcasted_iota(jnp.int32, (8, LANES), 1)
            expert = route_ref[4]
            chosen = ((lane == expert) | (lane == expert + LANES // 2)).astype(F32).astype(BF16)
            prob = lax.dot_general(
                chosen, held[:, 2 * width :], by_features, preferred_element_type=F32
            )[0:1]
        wait(2)
        hidden_grad = prob * product(down, held[:, width : 2 * width])
        sigmoid = jax.nn.sigmoid(gate_pre)
        active = gate_pre * sigmoid
        slope = sigmoid * (1.0 + gate_pre * (1.0 - sigmoid))
        stage[0, span] = (hidden_grad * up_pre * slope).astype(BF16)
        stage[1, span] = (hidden_grad * active).astype(BF16)
        stage[2, span] = (prob * active * up_pre).astype(BF16)
        for place in range(owners):
            if third * block < (place + 1) * share <= (third + 1) * block:
                for copy in flush(place):
                    copy.start()
    for place in range(owners):
        for copy in flush(place):
            copy.wait()


def hidden_rows(gathered, start, rows, route, w_gate, w_up, w_down):
    owners, share, width = w_gate.shape
    whole = pl.BlockSpec(memory_space=pl.ANY)
    kept = pltpu.VMEM((owners * share, width), BF16)
    return pl.pallas_call(
        functools.partial(hidden_kernel, start),
        grid_spec=pltpu.PrefetchScalarGridSpec(
            num_scalar_prefetch=1,
            grid=(1,),
            in_specs=[whole, whole, whole, whole],
            out_specs=[whole, whole, whole],
            scratch_shapes=[
                pltpu.VMEM((rows, gathered.shape[1]), BF16),
                kept,
                kept,
                kept,
                pltpu.VMEM((3, owners * share, rows), BF16),
                pltpu.SemaphoreType.DMA((2,)),
                pltpu.SemaphoreType.DMA((3, owners)),
                pltpu.SemaphoreType.DMA((owners, 3)),
            ],
        ),
        out_shape=[
            jax.ShapeDtypeStruct((3, owners, share, rows), BF16),
            jax.ShapeDtypeStruct((3, 2, share, rows), BF16),
            jax.ShapeDtypeStruct((3, 2, share, rows), BF16),
        ],
        compiler_params=pltpu.CompilerParams(vmem_limit_bytes=VMEM_LIMIT),
        cost_estimate=SMALL,
        name="hidden_rows",
    )(route, gathered, w_gate, w_up, w_down)


def input_kernel(core_ref, hidden_ref, gate_ref, up_ref, kept_ref, *rest):
    given_refs, turned = rest[:-1], rest[-1]
    count = pl.num_programs(0) // len(given_refs)

    @pl.when(pl.program_id(0) == 0)
    def _():
        turned[0] = hidden_ref[0].T
        turned[1] = hidden_ref[1].T

    total = jnp.dot(turned[0], gate_ref[...], preferred_element_type=F32)
    total += jnp.dot(turned[1], up_ref[...], preferred_element_type=F32)
    groups, share, step = kept_ref.shape
    total = total.astype(BF16).reshape(groups, 2, share, step)

    mine = core_ref[0] == 0
    kept_ref[...] = jnp.where(mine, total[:, 0], total[:, 1])
    for index, given_ref in enumerate(given_refs):

        @pl.when(pl.program_id(0) // count == index)
        def _():
            given_ref[...] = jnp.where(mine, total[:, 1], total[:, 0])


def input_rows(hidden, core, w_gate, w_up, share):
    _, units, token_count = hidden.shape
    width = w_gate.shape[1]
    step = 512
    groups = token_count // (2 * share)
    weight = pl.BlockSpec((units, step), lambda i, c: (0, i))
    part = pl.BlockSpec((groups, share, step), lambda i, c: (0, 0, i))
    shape = jax.ShapeDtypeStruct((groups, share, width), BF16)
    given_shape = jax.ShapeDtypeStruct((groups, share, width // GIVEN), BF16)
    count = width // step // GIVEN

    def given_part(index):
        return pl.BlockSpec(
            (groups, share, step),
            lambda i, c: (0, 0, jnp.clip(i - index * count, 0, count - 1)),
        )

    return pl.pallas_call(
        input_kernel,
        grid_spec=pltpu.PrefetchScalarGridSpec(
            num_scalar_prefetch=1,
            grid=(width // step,),
            in_specs=[pl.BlockSpec((2, units, token_count), lambda i, c: (0, 0, 0)), weight, weight],
            out_specs=[part] + [given_part(index) for index in range(GIVEN)],
            scratch_shapes=[pltpu.VMEM((2, token_count, units), BF16)],
        ),
        out_shape=[shape] + [given_shape] * GIVEN,
        compiler_params=pltpu.CompilerParams(vmem_limit_bytes=VMEM_LIMIT),
        cost_estimate=SMALL,
        name="input_rows",
    )(core, hidden, w_gate, w_up)


def pair_kernel(kept_ref, *refs):
    parts, out_ref = refs[:-1], refs[-1]
    step = parts[0].shape[2]
    for index, part in enumerate(parts):
        span = slice(index * step, (index + 1) * step)
        out_ref[:, :, span] = (kept_ref[:, :, span].astype(F32) + part[...].astype(F32)).astype(BF16)


def pair_sum(kept, parts):
    groups, share, width = kept.shape
    count = 4
    whole = pl.BlockSpec((groups // count, share, width), lambda i: (i, 0, 0))
    part = pl.BlockSpec((groups // count, share, width // len(parts)), lambda i: (i, 0, 0))
    return pl.pallas_call(
        pair_kernel,
        grid=(count,),
        in_specs=[whole] + [part] * len(parts),
        out_specs=whole,
        out_shape=jax.ShapeDtypeStruct(kept.shape, BF16),
        compiler_params=pltpu.CompilerParams(vmem_limit_bytes=VMEM_LIMIT),
        cost_estimate=SMALL,
        name="pair_sum",
    )(kept, *parts)


def own_kernel(
    pick_ref, first_ref, second_ref, tokens_ref, grads_ref, gate_ref, up_ref, down_ref, left
):
    share = first_ref.shape[2]

    @pl.when(pl.program_id(1) == 0)
    def _():
        for which in range(3):
            left[2 * share * which : 2 * share * which + share] = first_ref[which, 0]
            left[2 * share * which + share : 2 * share * (which + 1)] = second_ref[which, 0]

    both = jnp.dot(left[: 4 * share], tokens_ref[...], preferred_element_type=F32)
    gate_ref[0] = both[: 2 * share]
    up_ref[0] = both[2 * share :]
    down_ref[0] = jnp.dot(left[4 * share :], grads_ref[...], preferred_element_type=F32)


def own_grads(picks, hidden, gathered, width):
    _, _, share, token_count = hidden.shape
    step = 512
    count = width // 2 // step
    out = pl.BlockSpec((1, 2 * share, step), lambda h, i, p: (h, 0, i))
    shape = jax.ShapeDtypeStruct((2, 2 * share, width // 2), F32)
    return pl.pallas_call(
        own_kernel,
        grid_spec=pltpu.PrefetchScalarGridSpec(
            num_scalar_prefetch=1,
            grid=(2, count),
            in_specs=[
                pl.BlockSpec((3, 1, share, token_count), lambda h, i, p: (0, p[2 * h], 0, 0)),
                pl.BlockSpec((3, 1, share, token_count), lambda h, i, p: (0, p[2 * h + 1], 0, 0)),
                pl.BlockSpec((token_count, step), lambda h, i, p: (0, h * count + i)),
                pl.BlockSpec((token_count, step), lambda h, i, p: (0, (2 + h) * count + i)),
            ],
            out_specs=[out, out, out],
            scratch_shapes=[pltpu.VMEM((6 * share, token_count), BF16)],
        ),
        out_shape=[shape, shape, shape],
        compiler_params=pltpu.CompilerParams(vmem_limit_bytes=VMEM_LIMIT),
        cost_estimate=SMALL,
        name="own_grads",
    )(picks, hidden, hidden, gathered, gathered)


def weight_kernel(other_ref, near_ref, own_ref, out_first, out_second):
    share = out_first.shape[0]
    left = other_ref[0].reshape(2 * share, other_ref.shape[3])
    total = own_ref[0] + jnp.dot(left, near_ref[...], preferred_element_type=F32)
    out_first[...] = total[:share].astype(BF16)
    out_second[...] = total[share:].astype(BF16)


def weight_grads(which, half, other, gathered_near, own):
    _, _, share, token_count = other.shape
    columns = gathered_near.shape[1] // 4
    step = 512
    count = columns // step
    near_base = (half * 2 + which // 2) * count
    out = pl.BlockSpec((share, step), lambda i: (0, i))
    shape = jax.ShapeDtypeStruct((share, columns), BF16)
    return pl.pallas_call(
        weight_kernel,
        grid=(count,),
        in_specs=[
            pl.BlockSpec((1, 2, share, token_count), lambda i: (which, 0, 0, 0)),
            pl.BlockSpec((token_count, step), lambda i: (0, near_base + i)),
            pl.BlockSpec((1, 2 * share, step), lambda i: (half, 0, i)),
        ],
        out_specs=[out, out],
        out_shape=[shape, shape],
        compiler_params=pltpu.CompilerParams(vmem_limit_bytes=VMEM_LIMIT),
        cost_estimate=SMALL,
        name="weight_grads",
    )(other, gathered_near, own)


def per_device(tokens, out_grad, expert_ids, gate_probs, w_gate, w_up, w_down):
    token_count, width = tokens.shape
    half = width // 2
    owners = lax.axis_size("dp")
    ranks = lax.axis_size(("xl", "core"))
    experts = lax.axis_size(PLANE)
    units = w_gate.shape[1]
    share = token_count // ranks
    rank = lax.axis_index(("xl", "core"))
    core = lax.axis_index("core")
    expert = lax.axis_index(PLANE)
    place = lax.axis_index("dp")
    side = place ^ 1
    mirror = owners - 1 - place
    to_side = [(i, i ^ 1) for i in range(owners)]
    to_mirror = [(i, owners - 1 - i) for i in range(owners)]

    def own_share(array):
        return lax.dynamic_slice_in_dim(array, rank * share, share, 0)

    my_tokens, my_grads = own_share(tokens), own_share(out_grad)
    hits = own_share(expert_ids)[:, :, None] == jnp.arange(experts, dtype=jnp.int32)
    table = jnp.sum(jnp.where(hits, own_share(gate_probs)[:, :, None], 0.0), axis=1)
    coarse = table.astype(BF16)
    fine = (table - coarse.astype(F32)).astype(BF16)
    pad = jnp.zeros((share, LANES // 2 - experts), BF16)
    payload = jnp.concatenate([my_tokens, my_grads, coarse, pad, fine, pad], axis=1)
    gathered = lax.all_gather(payload, PLANE, axis=0, tiled=True)
    from_side = lax.ppermute(
        jnp.concatenate([my_tokens[:, :half], my_grads[:, :half]], axis=1), "dp", to_side
    )
    from_mirror = lax.ppermute(
        jnp.concatenate([my_tokens[:, half:], my_grads[:, half:]], axis=1), "dp", to_mirror
    )
    near_payload = jnp.concatenate([from_side, from_mirror], axis=1)
    gathered, near_payload = lax.optimization_barrier((gathered, near_payload))
    gathered_near = lax.all_gather(near_payload, PLANE, axis=0, tiled=True)

    route = jnp.stack([side, place ^ 2, mirror, place, expert]).astype(jnp.int32)
    gate, up, down = (w.reshape(owners, units // owners, width) for w in (w_gate, w_up, w_down))
    hidden, for_side, for_mirror = hidden_rows(
        gathered, 0, gathered.shape[0], route, gate, up, down
    )
    other_side = lax.ppermute(for_side, "dp", to_side)
    other_mirror = lax.ppermute(for_mirror, "dp", to_mirror)

    kept, *given = input_rows(
        hidden.reshape(3, units, -1), core[None], w_gate[0], w_up[0], share
    )
    picks = jnp.stack([place, mirror, side, place]).astype(jnp.int32)
    own = own_grads(picks, hidden, gathered, width)
    taken = [lax.ppermute(part, "core", [(0, 1), (1, 0)]) for part in given]
    paired = pair_sum(kept, taken)
    paired, own, other_side, other_mirror = lax.optimization_barrier(
        (paired, own, other_side, other_mirror)
    )
    returned = lax.all_to_all(paired, PLANE[:3], split_axis=0, concat_axis=0, tiled=True)

    mine, theirs = [], []
    for which in (2, 0, 1):
        mine_low, theirs_low = weight_grads(which, 0, other_side, gathered_near, own[which])
        theirs_high, mine_high = weight_grads(which, 1, other_mirror, gathered_near, own[which])
        mine.append((mine_low, mine_high))
        theirs.append((theirs_low, theirs_high))
    received = [
        (lax.ppermute(low, "dp", to_mirror), lax.ppermute(high, "dp", to_side)) for low, high in theirs
    ]
    results = []
    for (mine_low, mine_high), (low, high) in zip(mine, received):
        if len(results) == 2:
            returned, low, high, results = lax.optimization_barrier((returned, low, high, results))
        low = mine_low.astype(F32) + low.astype(F32)
        high = mine_high.astype(F32) + high.astype(F32)
        results.append(jnp.concatenate([low, high], axis=1).astype(BF16)[None])
    in_grad = jnp.sum(returned.astype(F32), axis=0).astype(BF16)
    return (in_grad, results[1], results[2], results[0])


def solution(mesh):
    dp, ctx, tensor = (mesh.shape[name] for name in ("dp", "ctx", "tensor"))
    fine = Mesh(
        mesh.devices.reshape(dp, ctx // 2, 2, tensor // 2, 2), ("dp", "z", "xh", "xl", "core")
    )
    token_spec = P(("dp", "z", "xh"), None)
    weight_spec = P(PLANE, None, None)
    grad_spec = P(PLANE, "dp", None)
    return jax.shard_map(
        per_device,
        mesh=fine,
        in_specs=(token_spec,) * 4 + (weight_spec,) * 3,
        out_specs=(P(("dp",) + PLANE, None), grad_spec, grad_spec, grad_spec),
        check_vma=False,
    )
```

```python
import functools

import jax
import jax.numpy as jnp
from jax import lax
from jax.experimental import pallas as pl
from jax.experimental.pallas import tpu as pltpu
from jax.sharding import Mesh
from jax.sharding import PartitionSpec as P

BF16 = jnp.bfloat16
F32 = jnp.float32
VMEM_LIMIT = 56 * 1024 * 1024
PLANE = ("z", "xh", "xl", "core")
LANES = 128
GIVEN = 4
SMALL = pl.CostEstimate(flops=0, bytes_accessed=0, transcendentals=0)


def hidden_kernel(
    start, route_ref, gathered_ref, gate_ref, up_ref, down_ref, out_ref, near_ref, far_ref,
    held, gate, up, down, stage, token_sems, weight_sems, out_sems,
):
    rows = stage.shape[2]
    owners, share, width = gate_ref.shape
    block = 256
    weights = ((gate_ref, gate), (up_ref, up), (down_ref, down))

    def token_copy(part):
        columns = pl.ds(0, width) if part == 0 else pl.ds(width, held.shape[1] - width)
        return pltpu.make_async_copy(
            gathered_ref.at[pl.ds(start, rows), columns], held.at[:, columns], token_sems.at[part]
        )

    def weight_copy(which, place):
        source, target = weights[which]
        return pltpu.make_async_copy(
            source.at[route_ref[place]],
            target.at[pl.ds(place * share, share)],
            weight_sems.at[which, place],
        )

    token_copy(0).start()
    for which in range(3):
        if which == 2:
            token_copy(1).start()
        weight_copy(which, 0).start()
        weight_copy(which, 1).start()
    for place in range(2, owners):
        for which in range(3):
            weight_copy(which, place).start()

    def flush(place):
        source = stage.at[:, pl.ds(place * share, share)]
        targets = [out_ref.at[:, route_ref[place]]]
        if place < 2:
            targets.append(near_ref.at[:, place])
        if 0 < place < 3:
            targets.append(far_ref.at[:, place - 1])
        return [
            pltpu.make_async_copy(source, target, out_sems.at[place, index])
            for index, target in enumerate(targets)
        ]

    by_features = (((1,), (1,)), ((), ()))
    for third in range(3):
        span = pl.ds(third * block, block)

        def wait(which):
            if third == 0:
                weight_copy(which, 0).wait()
                weight_copy(which, 1).wait()
            else:
                weight_copy(which, third + 1).wait()

        def product(array, right):
            return lax.dot_general(array[span], right, by_features, preferred_element_type=F32)

        if third == 0:
            token_copy(0).wait()
        wait(0)
        gate_pre = product(gate, held[:, :width])
        wait(1)
        up_pre = product(up, held[:, :width])
        if third == 0:
            token_copy(1).wait()
            lane = lax.broadcasted_iota(jnp.int32, (8, LANES), 1)
            expert = route_ref[4]
            chosen = ((lane == expert) | (lane == expert + LANES // 2)).astype(F32).astype(BF16)
            prob = lax.dot_general(
                chosen, held[:, 2 * width :], by_features, preferred_element_type=F32
            )[0:1]
        wait(2)
        hidden_grad = prob * product(down, held[:, width : 2 * width])
        sigmoid = jax.nn.sigmoid(gate_pre)
        active = gate_pre * sigmoid
        slope = sigmoid * (1.0 + gate_pre * (1.0 - sigmoid))
        stage[0, span] = (hidden_grad * up_pre * slope).astype(BF16)
        stage[1, span] = (hidden_grad * active).astype(BF16)
        stage[2, span] = (prob * active * up_pre).astype(BF16)
        for place in range(owners):
            if third * block < (place + 1) * share <= (third + 1) * block:
                for copy in flush(place):
                    copy.start()
    for place in range(owners):
        for copy in flush(place):
            copy.wait()


def hidden_rows(gathered, start, rows, route, w_gate, w_up, w_down):
    owners, share, width = w_gate.shape
    whole = pl.BlockSpec(memory_space=pl.ANY)
    kept = pltpu.VMEM((owners * share, width), BF16)
    return pl.pallas_call(
        functools.partial(hidden_kernel, start),
        grid_spec=pltpu.PrefetchScalarGridSpec(
            num_scalar_prefetch=1,
            grid=(1,),
            in_specs=[whole, whole, whole, whole],
            out_specs=[whole, whole, whole],
            scratch_shapes=[
                pltpu.VMEM((rows, gathered.shape[1]), BF16),
                kept,
                kept,
                kept,
                pltpu.VMEM((3, owners * share, rows), BF16),
                pltpu.SemaphoreType.DMA((2,)),
                pltpu.SemaphoreType.DMA((3, owners)),
                pltpu.SemaphoreType.DMA((owners, 3)),
            ],
        ),
        out_shape=[
            jax.ShapeDtypeStruct((3, owners, share, rows), BF16),
            jax.ShapeDtypeStruct((3, 2, share, rows), BF16),
            jax.ShapeDtypeStruct((3, 2, share, rows), BF16),
        ],
        compiler_params=pltpu.CompilerParams(vmem_limit_bytes=VMEM_LIMIT),
        cost_estimate=SMALL,
        name="hidden_rows",
    )(route, gathered, w_gate, w_up, w_down)


def input_kernel(core_ref, hidden_ref, gate_ref, up_ref, kept_ref, *rest):
    given_refs, turned = rest[:-1], rest[-1]
    count = pl.num_programs(0) // len(given_refs)

    @pl.when(pl.program_id(0) == 0)
    def _():
        turned[0] = hidden_ref[0].T
        turned[1] = hidden_ref[1].T

    total = jnp.dot(turned[0], gate_ref[...], preferred_element_type=F32)
    total += jnp.dot(turned[1], up_ref[...], preferred_element_type=F32)
    groups, share, step = kept_ref.shape
    total = total.astype(BF16).reshape(groups, 2, share, step)

    mine = core_ref[0] == 0
    kept_ref[...] = jnp.where(mine, total[:, 0], total[:, 1])
    for index, given_ref in enumerate(given_refs):

        @pl.when(pl.program_id(0) // count == index)
        def _():
            given_ref[...] = jnp.where(mine, total[:, 1], total[:, 0])


def input_rows(hidden, core, w_gate, w_up, share):
    _, units, token_count = hidden.shape
    width = w_gate.shape[1]
    step = 512
    groups = token_count // (2 * share)
    weight = pl.BlockSpec((units, step), lambda i, c: (0, i))
    part = pl.BlockSpec((groups, share, step), lambda i, c: (0, 0, i))
    shape = jax.ShapeDtypeStruct((groups, share, width), BF16)
    given_shape = jax.ShapeDtypeStruct((groups, share, width // GIVEN), BF16)
    count = width // step // GIVEN

    def given_part(index):
        return pl.BlockSpec(
            (groups, share, step),
            lambda i, c: (0, 0, jnp.clip(i - index * count, 0, count - 1)),
        )

    return pl.pallas_call(
        input_kernel,
        grid_spec=pltpu.PrefetchScalarGridSpec(
            num_scalar_prefetch=1,
            grid=(width // step,),
            in_specs=[pl.BlockSpec((2, units, token_count), lambda i, c: (0, 0, 0)), weight, weight],
            out_specs=[part] + [given_part(index) for index in range(GIVEN)],
            scratch_shapes=[pltpu.VMEM((2, token_count, units), BF16)],
        ),
        out_shape=[shape] + [given_shape] * GIVEN,
        compiler_params=pltpu.CompilerParams(vmem_limit_bytes=VMEM_LIMIT),
        cost_estimate=SMALL,
        name="input_rows",
    )(core, hidden, w_gate, w_up)


def pair_kernel(kept_ref, *refs):
    parts, out_ref = refs[:-1], refs[-1]
    step = parts[0].shape[2]
    for index, part in enumerate(parts):
        span = slice(index * step, (index + 1) * step)
        out_ref[:, :, span] = (kept_ref[:, :, span].astype(F32) + part[...].astype(F32)).astype(BF16)


def pair_sum(kept, parts):
    groups, share, width = kept.shape
    count = 4
    whole = pl.BlockSpec((groups // count, share, width), lambda i: (i, 0, 0))
    part = pl.BlockSpec((groups // count, share, width // len(parts)), lambda i: (i, 0, 0))
    return pl.pallas_call(
        pair_kernel,
        grid=(count,),
        in_specs=[whole] + [part] * len(parts),
        out_specs=whole,
        out_shape=jax.ShapeDtypeStruct(kept.shape, BF16),
        compiler_params=pltpu.CompilerParams(vmem_limit_bytes=VMEM_LIMIT),
        cost_estimate=SMALL,
        name="pair_sum",
    )(kept, *parts)


def own_kernel(
    pick_ref, first_ref, second_ref, tokens_ref, grads_ref, gate_ref, up_ref, down_ref, left
):
    share = first_ref.shape[2]

    @pl.when(pl.program_id(1) == 0)
    def _():
        for which in range(3):
            left[2 * share * which : 2 * share * which + share] = first_ref[which, 0]
            left[2 * share * which + share : 2 * share * (which + 1)] = second_ref[which, 0]

    both = jnp.dot(left[: 4 * share], tokens_ref[...], preferred_element_type=F32)
    gate_ref[0] = both[: 2 * share].astype(BF16)
    up_ref[0] = both[2 * share :].astype(BF16)
    down_ref[0] = jnp.dot(
        left[4 * share :], grads_ref[...], preferred_element_type=F32
    ).astype(BF16)


def own_grads(picks, hidden, gathered, width):
    _, _, share, token_count = hidden.shape
    step = 512
    count = width // 2 // step
    out = pl.BlockSpec((1, 2 * share, step), lambda h, i, p: (h, 0, i))
    shape = jax.ShapeDtypeStruct((2, 2 * share, width // 2), BF16)
    return pl.pallas_call(
        own_kernel,
        grid_spec=pltpu.PrefetchScalarGridSpec(
            num_scalar_prefetch=1,
            grid=(2, count),
            in_specs=[
                pl.BlockSpec((3, 1, share, token_count), lambda h, i, p: (0, p[2 * h], 0, 0)),
                pl.BlockSpec((3, 1, share, token_count), lambda h, i, p: (0, p[2 * h + 1], 0, 0)),
                pl.BlockSpec((token_count, step), lambda h, i, p: (0, h * count + i)),
                pl.BlockSpec((token_count, step), lambda h, i, p: (0, (2 + h) * count + i)),
            ],
            out_specs=[out, out, out],
            scratch_shapes=[pltpu.VMEM((6 * share, token_count), BF16)],
        ),
        out_shape=[shape, shape, shape],
        compiler_params=pltpu.CompilerParams(vmem_limit_bytes=VMEM_LIMIT),
        cost_estimate=SMALL,
        name="own_grads",
    )(picks, hidden, hidden, gathered, gathered)


def weight_kernel(other_ref, near_ref, own_ref, out_first, out_second):
    share = out_first.shape[0]
    left = other_ref[0].reshape(2 * share, other_ref.shape[3])
    total = own_ref[0].astype(F32) + jnp.dot(left, near_ref[...], preferred_element_type=F32)
    out_first[...] = total[:share].astype(BF16)
    out_second[...] = total[share:].astype(BF16)


def weight_grads(which, half, other, gathered_near, own):
    _, _, share, token_count = other.shape
    columns = gathered_near.shape[1] // 4
    step = 512
    count = columns // step
    near_base = (half * 2 + which // 2) * count
    out = pl.BlockSpec((share, step), lambda i: (0, i))
    shape = jax.ShapeDtypeStruct((share, columns), BF16)
    return pl.pallas_call(
        weight_kernel,
        grid=(count,),
        in_specs=[
            pl.BlockSpec((1, 2, share, token_count), lambda i: (which, 0, 0, 0)),
            pl.BlockSpec((token_count, step), lambda i: (0, near_base + i)),
            pl.BlockSpec((1, 2 * share, step), lambda i: (half, 0, i)),
        ],
        out_specs=[out, out],
        out_shape=[shape, shape],
        compiler_params=pltpu.CompilerParams(vmem_limit_bytes=VMEM_LIMIT),
        cost_estimate=SMALL,
        name="weight_grads",
    )(other, gathered_near, own)


def per_device(tokens, out_grad, expert_ids, gate_probs, w_gate, w_up, w_down):
    token_count, width = tokens.shape
    half = width // 2
    owners = lax.axis_size("dp")
    ranks = lax.axis_size(("xl", "core"))
    experts = lax.axis_size(PLANE)
    units = w_gate.shape[1]
    share = token_count // ranks
    rank = lax.axis_index(("xl", "core"))
    core = lax.axis_index("core")
    expert = lax.axis_index(PLANE)
    place = lax.axis_index("dp")
    side = place ^ 1
    mirror = owners - 1 - place
    to_side = [(i, i ^ 1) for i in range(owners)]
    to_mirror = [(i, owners - 1 - i) for i in range(owners)]

    def own_share(array):
        return lax.dynamic_slice_in_dim(array, rank * share, share, 0)

    my_tokens, my_grads = own_share(tokens), own_share(out_grad)
    hits = own_share(expert_ids)[:, :, None] == jnp.arange(experts, dtype=jnp.int32)
    table = jnp.sum(jnp.where(hits, own_share(gate_probs)[:, :, None], 0.0), axis=1)
    coarse = table.astype(BF16)
    fine = (table - coarse.astype(F32)).astype(BF16)
    pad = jnp.zeros((share, LANES // 2 - experts), BF16)
    payload = jnp.concatenate([my_tokens, my_grads, coarse, pad, fine, pad], axis=1)
    gathered = lax.all_gather(payload, PLANE, axis=0, tiled=True)
    from_side = lax.ppermute(
        jnp.concatenate([my_tokens[:, :half], my_grads[:, :half]], axis=1), "dp", to_side
    )
    from_mirror = lax.ppermute(
        jnp.concatenate([my_tokens[:, half:], my_grads[:, half:]], axis=1), "dp", to_mirror
    )
    near_payload = jnp.concatenate([from_side, from_mirror], axis=1)
    gathered, near_payload = lax.optimization_barrier((gathered, near_payload))
    gathered_near = lax.all_gather(near_payload, PLANE, axis=0, tiled=True)

    route = jnp.stack([side, place ^ 2, mirror, place, expert]).astype(jnp.int32)
    gate, up, down = (w.reshape(owners, units // owners, width) for w in (w_gate, w_up, w_down))
    hidden, for_side, for_mirror = hidden_rows(
        gathered, 0, gathered.shape[0], route, gate, up, down
    )
    other_side = lax.ppermute(for_side, "dp", to_side)
    other_mirror = lax.ppermute(for_mirror, "dp", to_mirror)

    kept, *given = input_rows(
        hidden.reshape(3, units, -1), core[None], w_gate[0], w_up[0], share
    )
    picks = jnp.stack([place, mirror, side, place]).astype(jnp.int32)
    own = own_grads(picks, hidden, gathered, width)
    taken = [lax.ppermute(part, "core", [(0, 1), (1, 0)]) for part in given]
    paired = pair_sum(kept, taken)
    paired, own, other_side, other_mirror = lax.optimization_barrier(
        (paired, own, other_side, other_mirror)
    )
    returned = lax.all_to_all(paired, PLANE[:3], split_axis=0, concat_axis=0, tiled=True)

    mine, theirs = [], []
    for which in (2, 0, 1):
        mine_low, theirs_low = weight_grads(which, 0, other_side, gathered_near, own[which])
        theirs_high, mine_high = weight_grads(which, 1, other_mirror, gathered_near, own[which])
        mine.append((mine_low, mine_high))
        theirs.append((theirs_low, theirs_high))
    received = [
        (lax.ppermute(low, "dp", to_mirror), lax.ppermute(high, "dp", to_side)) for low, high in theirs
    ]
    results = []
    for (mine_low, mine_high), (low, high) in zip(mine, received):
        if len(results) == 2:
            returned, low, high, results = lax.optimization_barrier((returned, low, high, results))
        low = mine_low.astype(F32) + low.astype(F32)
        high = mine_high.astype(F32) + high.astype(F32)
        results.append(jnp.concatenate([low, high], axis=1).astype(BF16)[None])
    in_grad = jnp.sum(returned.astype(F32), axis=0).astype(BF16)
    return (in_grad, results[1], results[2], results[0])


def solution(mesh):
    dp, ctx, tensor = (mesh.shape[name] for name in ("dp", "ctx", "tensor"))
    fine = Mesh(
        mesh.devices.reshape(dp, ctx // 2, 2, tensor // 2, 2), ("dp", "z", "xh", "xl", "core")
    )
    token_spec = P(("dp", "z", "xh"), None)
    weight_spec = P(PLANE, None, None)
    grad_spec = P(PLANE, "dp", None)
    return jax.shard_map(
        per_device,
        mesh=fine,
        in_specs=(token_spec,) * 4 + (weight_spec,) * 3,
        out_specs=(P(("dp",) + PLANE, None), grad_spec, grad_spec, grad_spec),
        check_vma=False,
    )
```

```python
import functools

import jax
import jax.numpy as jnp
from jax import lax
from jax.experimental import pallas as pl
from jax.experimental.pallas import tpu as pltpu
from jax.sharding import Mesh
from jax.sharding import PartitionSpec as P

BF16 = jnp.bfloat16
F32 = jnp.float32
VMEM_LIMIT = 56 * 1024 * 1024
PLANE = ("z", "xh", "xl", "core")
LANES = 128
GIVEN = 4
SMALL = pl.CostEstimate(flops=0, bytes_accessed=0, transcendentals=0)


def hidden_kernel(
    start, route_ref, gathered_ref, gate_ref, up_ref, down_ref, out_ref, near_ref, far_ref,
    held, gate, up, down, stage, token_sems, weight_sems, out_sems,
):
    rows = stage.shape[2]
    owners, share, width = gate_ref.shape
    block = 256
    weights = ((gate_ref, gate), (up_ref, up), (down_ref, down))

    def token_copy(part):
        columns = pl.ds(0, width) if part == 0 else pl.ds(width, held.shape[1] - width)
        return pltpu.make_async_copy(
            gathered_ref.at[pl.ds(start, rows), columns], held.at[:, columns], token_sems.at[part]
        )

    def weight_copy(which, place):
        source, target = weights[which]
        return pltpu.make_async_copy(
            source.at[route_ref[place]],
            target.at[pl.ds(place * share, share)],
            weight_sems.at[which, place],
        )

    token_copy(0).start()
    for which in range(3):
        if which == 2:
            token_copy(1).start()
        weight_copy(which, 0).start()
        weight_copy(which, 1).start()
    for place in range(2, owners):
        for which in range(3):
            weight_copy(which, place).start()

    def flush(place):
        source = stage.at[:, pl.ds(place * share, share)]
        targets = [out_ref.at[:, route_ref[place]]]
        if place < 2:
            targets.append(near_ref.at[:, place])
        if 0 < place < 3:
            targets.append(far_ref.at[:, place - 1])
        return [
            pltpu.make_async_copy(source, target, out_sems.at[place, index])
            for index, target in enumerate(targets)
        ]

    by_features = (((1,), (1,)), ((), ()))
    for third in range(3):
        span = pl.ds(third * block, block)

        def wait(which):
            if third == 0:
                weight_copy(which, 0).wait()
                weight_copy(which, 1).wait()
            else:
                weight_copy(which, third + 1).wait()

        def product(array, right):
            return lax.dot_general(array[span], right, by_features, preferred_element_type=F32)

        if third == 0:
            token_copy(0).wait()
        wait(0)
        gate_pre = product(gate, held[:, :width])
        wait(1)
        up_pre = product(up, held[:, :width])
        if third == 0:
            token_copy(1).wait()
            lane = lax.broadcasted_iota(jnp.int32, (8, LANES), 1)
            expert = route_ref[4]
            chosen = ((lane == expert) | (lane == expert + LANES // 2)).astype(F32).astype(BF16)
            prob = lax.dot_general(
                chosen, held[:, 2 * width :], by_features, preferred_element_type=F32
            )[0:1]
        wait(2)
        hidden_grad = prob * product(down, held[:, width : 2 * width])
        sigmoid = jax.nn.sigmoid(gate_pre)
        active = gate_pre * sigmoid
        slope = sigmoid * (1.0 + gate_pre * (1.0 - sigmoid))
        stage[0, span] = (hidden_grad * up_pre * slope).astype(BF16)
        stage[1, span] = (hidden_grad * active).astype(BF16)
        stage[2, span] = (prob * active * up_pre).astype(BF16)
        for place in range(owners):
            if third * block < (place + 1) * share <= (third + 1) * block:
                for copy in flush(place):
                    copy.start()
    for place in range(owners):
        for copy in flush(place):
            copy.wait()


def hidden_rows(gathered, start, rows, route, w_gate, w_up, w_down):
    owners, share, width = w_gate.shape
    whole = pl.BlockSpec(memory_space=pl.ANY)
    kept = pltpu.VMEM((owners * share, width), BF16)
    return pl.pallas_call(
        functools.partial(hidden_kernel, start),
        grid_spec=pltpu.PrefetchScalarGridSpec(
            num_scalar_prefetch=1,
            grid=(1,),
            in_specs=[whole, whole, whole, whole],
            out_specs=[whole, whole, whole],
            scratch_shapes=[
                pltpu.VMEM((rows, gathered.shape[1]), BF16),
                kept,
                kept,
                kept,
                pltpu.VMEM((3, owners * share, rows), BF16),
                pltpu.SemaphoreType.DMA((2,)),
                pltpu.SemaphoreType.DMA((3, owners)),
                pltpu.SemaphoreType.DMA((owners, 3)),
            ],
        ),
        out_shape=[
            jax.ShapeDtypeStruct((3, owners, share, rows), BF16),
            jax.ShapeDtypeStruct((3, 2, share, rows), BF16),
            jax.ShapeDtypeStruct((3, 2, share, rows), BF16),
        ],
        compiler_params=pltpu.CompilerParams(vmem_limit_bytes=VMEM_LIMIT),
        cost_estimate=SMALL,
        name="hidden_rows",
    )(route, gathered, w_gate, w_up, w_down)


def input_kernel(core_ref, hidden_ref, gate_ref, up_ref, kept_ref, *rest):
    given_refs, turned = rest[:-1], rest[-1]
    count = pl.num_programs(0) // len(given_refs)

    @pl.when(pl.program_id(0) == 0)
    def _():
        turned[0] = hidden_ref[0].T
        turned[1] = hidden_ref[1].T

    total = jnp.dot(turned[0], gate_ref[...], preferred_element_type=F32)
    total += jnp.dot(turned[1], up_ref[...], preferred_element_type=F32)
    groups, share, step = kept_ref.shape
    total = total.astype(BF16).reshape(groups, 2, share, step)

    mine = core_ref[0] == 0
    kept_ref[...] = jnp.where(mine, total[:, 0], total[:, 1])
    for index, given_ref in enumerate(given_refs):

        @pl.when(pl.program_id(0) // count == index)
        def _():
            given_ref[...] = jnp.where(mine, total[:, 1], total[:, 0])


def input_rows(hidden, core, w_gate, w_up, share):
    _, units, token_count = hidden.shape
    width = w_gate.shape[1]
    step = 512
    groups = token_count // (2 * share)
    weight = pl.BlockSpec((units, step), lambda i, c: (0, i))
    part = pl.BlockSpec((groups, share, step), lambda i, c: (0, 0, i))
    shape = jax.ShapeDtypeStruct((groups, share, width), BF16)
    given_shape = jax.ShapeDtypeStruct((groups, share, width // GIVEN), BF16)
    count = width // step // GIVEN

    def given_part(index):
        return pl.BlockSpec(
            (groups, share, step),
            lambda i, c: (0, 0, jnp.clip(i - index * count, 0, count - 1)),
        )

    return pl.pallas_call(
        input_kernel,
        grid_spec=pltpu.PrefetchScalarGridSpec(
            num_scalar_prefetch=1,
            grid=(width // step,),
            in_specs=[pl.BlockSpec((2, units, token_count), lambda i, c: (0, 0, 0)), weight, weight],
            out_specs=[part] + [given_part(index) for index in range(GIVEN)],
            scratch_shapes=[pltpu.VMEM((2, token_count, units), BF16)],
        ),
        out_shape=[shape] + [given_shape] * GIVEN,
        compiler_params=pltpu.CompilerParams(vmem_limit_bytes=VMEM_LIMIT),
        cost_estimate=SMALL,
        name="input_rows",
    )(core, hidden, w_gate, w_up)


def pair_kernel(kept_ref, *refs):
    parts, out_ref = refs[:-1], refs[-1]
    step = parts[0].shape[2]
    for index, part in enumerate(parts):
        span = slice(index * step, (index + 1) * step)
        out_ref[:, :, span] = (kept_ref[:, :, span].astype(F32) + part[...].astype(F32)).astype(BF16)


def pair_sum(kept, parts):
    groups, share, width = kept.shape
    count = 4
    whole = pl.BlockSpec((groups // count, share, width), lambda i: (i, 0, 0))
    part = pl.BlockSpec((groups // count, share, width // len(parts)), lambda i: (i, 0, 0))
    return pl.pallas_call(
        pair_kernel,
        grid=(count,),
        in_specs=[whole] + [part] * len(parts),
        out_specs=whole,
        out_shape=jax.ShapeDtypeStruct(kept.shape, BF16),
        compiler_params=pltpu.CompilerParams(vmem_limit_bytes=VMEM_LIMIT),
        cost_estimate=SMALL,
        name="pair_sum",
    )(kept, *parts)


def own_kernel(
    pick_ref, first_ref, second_ref, tokens_ref, grads_ref, gate_ref, up_ref, down_ref, left
):
    share = first_ref.shape[2]

    @pl.when(pl.program_id(1) == 0)
    def _():
        for which in range(3):
            left[2 * share * which : 2 * share * which + share] = first_ref[which, 0]
            left[2 * share * which + share : 2 * share * (which + 1)] = second_ref[which, 0]

    both = jnp.dot(left[: 4 * share], tokens_ref[...], preferred_element_type=F32)
    gate_ref[0] = both[: 2 * share].astype(BF16)
    up_ref[0] = both[2 * share :].astype(BF16)
    down_ref[0] = jnp.dot(
        left[4 * share :], grads_ref[...], preferred_element_type=F32
    ).astype(BF16)


def own_grads(picks, hidden, gathered, width):
    _, _, share, token_count = hidden.shape
    step = 512
    count = width // 2 // step
    out = pl.BlockSpec((1, 2 * share, step), lambda h, i, p: (h, 0, i))
    shape = jax.ShapeDtypeStruct((2, 2 * share, width // 2), BF16)
    return pl.pallas_call(
        own_kernel,
        grid_spec=pltpu.PrefetchScalarGridSpec(
            num_scalar_prefetch=1,
            grid=(2, count),
            in_specs=[
                pl.BlockSpec((3, 1, share, token_count), lambda h, i, p: (0, p[2 * h], 0, 0)),
                pl.BlockSpec((3, 1, share, token_count), lambda h, i, p: (0, p[2 * h + 1], 0, 0)),
                pl.BlockSpec((token_count, step), lambda h, i, p: (0, h * count + i)),
                pl.BlockSpec((token_count, step), lambda h, i, p: (0, (2 + h) * count + i)),
            ],
            out_specs=[out, out, out],
            scratch_shapes=[pltpu.VMEM((6 * share, token_count), BF16)],
        ),
        out_shape=[shape, shape, shape],
        compiler_params=pltpu.CompilerParams(vmem_limit_bytes=VMEM_LIMIT),
        cost_estimate=SMALL,
        name="own_grads",
    )(picks, hidden, hidden, gathered, gathered)


def weight_kernel(other_ref, near_ref, own_ref, out_first, out_second):
    share = out_first.shape[0]
    left = other_ref[0].reshape(2 * share, other_ref.shape[3])
    total = own_ref[0].astype(F32) + jnp.dot(left, near_ref[...], preferred_element_type=F32)
    out_first[...] = total[:share].astype(BF16)
    out_second[...] = total[share:].astype(BF16)


def weight_grads(which, half, other, gathered_near, own):
    _, _, share, token_count = other.shape
    columns = gathered_near.shape[1] // 4
    step = 512
    count = columns // step
    near_base = (half * 2 + which // 2) * count
    out = pl.BlockSpec((share, step), lambda i: (0, i))
    shape = jax.ShapeDtypeStruct((share, columns), BF16)
    return pl.pallas_call(
        weight_kernel,
        grid=(count,),
        in_specs=[
            pl.BlockSpec((1, 2, share, token_count), lambda i: (which, 0, 0, 0)),
            pl.BlockSpec((token_count, step), lambda i: (0, near_base + i)),
            pl.BlockSpec((1, 2 * share, step), lambda i: (half, 0, i)),
        ],
        out_specs=[out, out],
        out_shape=[shape, shape],
        compiler_params=pltpu.CompilerParams(vmem_limit_bytes=VMEM_LIMIT),
        cost_estimate=SMALL,
        name="weight_grads",
    )(other, gathered_near, own)


def per_device(tokens, out_grad, expert_ids, gate_probs, w_gate, w_up, w_down):
    token_count, width = tokens.shape
    half = width // 2
    owners = lax.axis_size("dp")
    ranks = lax.axis_size(("xl", "core"))
    experts = lax.axis_size(PLANE)
    units = w_gate.shape[1]
    share = token_count // ranks
    rank = lax.axis_index(("xl", "core"))
    core = lax.axis_index("core")
    expert = lax.axis_index(PLANE)
    place = lax.axis_index("dp")
    side = place ^ 1
    mirror = owners - 1 - place
    to_side = [(i, i ^ 1) for i in range(owners)]
    to_mirror = [(i, owners - 1 - i) for i in range(owners)]

    def own_share(array):
        return lax.dynamic_slice_in_dim(array, rank * share, share, 0)

    my_tokens, my_grads = own_share(tokens), own_share(out_grad)
    hits = own_share(expert_ids)[:, :, None] == jnp.arange(experts, dtype=jnp.int32)
    table = jnp.sum(jnp.where(hits, own_share(gate_probs)[:, :, None], 0.0), axis=1)
    coarse = table.astype(BF16)
    fine = (table - coarse.astype(F32)).astype(BF16)
    pad = jnp.zeros((share, LANES // 2 - experts), BF16)
    payload = jnp.concatenate([my_tokens, my_grads, coarse, pad, fine, pad], axis=1)
    gathered = lax.all_gather(payload, PLANE, axis=0, tiled=True)
    from_side = lax.ppermute(
        jnp.concatenate([my_tokens[:, :half], my_grads[:, :half]], axis=1), "dp", to_side
    )
    from_mirror = lax.ppermute(
        jnp.concatenate([my_tokens[:, half:], my_grads[:, half:]], axis=1), "dp", to_mirror
    )
    near_payload = jnp.concatenate([from_side, from_mirror], axis=1)
    gathered, near_payload = lax.optimization_barrier((gathered, near_payload))
    gathered_near = lax.all_gather(near_payload, PLANE, axis=0, tiled=True)

    route = jnp.stack([side, place ^ 2, mirror, place, expert]).astype(jnp.int32)
    gate, up, down = (w.reshape(owners, units // owners, width) for w in (w_gate, w_up, w_down))
    hidden, for_side, for_mirror = hidden_rows(
        gathered, 0, gathered.shape[0], route, gate, up, down
    )
    other_side = lax.ppermute(for_side, "dp", to_side)
    other_mirror = lax.ppermute(for_mirror, "dp", to_mirror)

    kept, *given = input_rows(
        hidden.reshape(3, units, -1), core[None], w_gate[0], w_up[0], share
    )
    picks = jnp.stack([place, mirror, side, place]).astype(jnp.int32)
    own = own_grads(picks, hidden, gathered, width)
    taken = [lax.ppermute(part, "core", [(0, 1), (1, 0)]) for part in given]
    paired = pair_sum(kept, taken)
    paired, own, other_side, other_mirror = lax.optimization_barrier(
        (paired, own, other_side, other_mirror)
    )
    returned = lax.all_to_all(paired, PLANE[:3], split_axis=0, concat_axis=0, tiled=True)

    mine, theirs = [], []
    for which in (2, 0, 1):
        mine_low, theirs_low = weight_grads(which, 0, other_side, gathered_near, own[which])
        theirs_high, mine_high = weight_grads(which, 1, other_mirror, gathered_near, own[which])
        mine.append((mine_low, mine_high))
        theirs.append((theirs_low, theirs_high))
    received = [
        (lax.ppermute(low, "dp", to_mirror), lax.ppermute(high, "dp", to_side)) for low, high in theirs
    ]
    results = []
    for (mine_low, mine_high), (low, high) in zip(mine, received):
        if len(results) == 2:
            returned, results = lax.optimization_barrier((returned, results))
        low = mine_low.astype(F32) + low.astype(F32)
        high = mine_high.astype(F32) + high.astype(F32)
        results.append(jnp.concatenate([low, high], axis=1).astype(BF16)[None])
    in_grad = jnp.sum(returned.astype(F32), axis=0).astype(BF16)
    return (in_grad, results[1], results[2], results[0])


def solution(mesh):
    dp, ctx, tensor = (mesh.shape[name] for name in ("dp", "ctx", "tensor"))
    fine = Mesh(
        mesh.devices.reshape(dp, ctx // 2, 2, tensor // 2, 2), ("dp", "z", "xh", "xl", "core")
    )
    token_spec = P(("dp", "z", "xh"), None)
    weight_spec = P(PLANE, None, None)
    grad_spec = P(PLANE, "dp", None)
    return jax.shard_map(
        per_device,
        mesh=fine,
        in_specs=(token_spec,) * 4 + (weight_spec,) * 3,
        out_specs=(P(("dp",) + PLANE, None), grad_spec, grad_spec, grad_spec),
        check_vma=False,
    )
```

```python
import functools

import jax
import jax.numpy as jnp
from jax import lax
from jax.experimental import pallas as pl
from jax.experimental.pallas import tpu as pltpu
from jax.sharding import Mesh
from jax.sharding import PartitionSpec as P

BF16 = jnp.bfloat16
F32 = jnp.float32
VMEM_LIMIT = 56 * 1024 * 1024
PLANE = ("z", "xh", "xl", "core")
LANES = 128
GIVEN = 4
SMALL = pl.CostEstimate(flops=0, bytes_accessed=0, transcendentals=0)


def hidden_kernel(
    start, route_ref, gathered_ref, gate_ref, up_ref, down_ref, out_ref, near_ref, far_ref,
    held, gate, up, down, stage, token_sems, weight_sems, out_sems,
):
    rows = stage.shape[2]
    owners, share, width = gate_ref.shape
    block = 256
    weights = ((gate_ref, gate), (up_ref, up), (down_ref, down))

    def token_copy(part):
        columns = pl.ds(0, width) if part == 0 else pl.ds(width, held.shape[1] - width)
        return pltpu.make_async_copy(
            gathered_ref.at[pl.ds(start, rows), columns], held.at[:, columns], token_sems.at[part]
        )

    def weight_copy(which, place):
        source, target = weights[which]
        return pltpu.make_async_copy(
            source.at[route_ref[place]],
            target.at[pl.ds(place * share, share)],
            weight_sems.at[which, place],
        )

    token_copy(0).start()
    for which in range(3):
        if which == 2:
            token_copy(1).start()
        weight_copy(which, 0).start()
        weight_copy(which, 1).start()
    for place in range(2, owners):
        for which in range(3):
            weight_copy(which, place).start()

    def flush(place):
        source = stage.at[:, pl.ds(place * share, share)]
        targets = [out_ref.at[:, route_ref[place]]]
        if place < 2:
            targets.append(near_ref.at[:, place])
        if 0 < place < 3:
            targets.append(far_ref.at[:, place - 1])
        return [
            pltpu.make_async_copy(source, target, out_sems.at[place, index])
            for index, target in enumerate(targets)
        ]

    by_features = (((1,), (1,)), ((), ()))
    for third in range(3):
        span = pl.ds(third * block, block)

        def wait(which):
            if third == 0:
                weight_copy(which, 0).wait()
                weight_copy(which, 1).wait()
            else:
                weight_copy(which, third + 1).wait()

        def product(array, right):
            return lax.dot_general(array[span], right, by_features, preferred_element_type=F32)

        if third == 0:
            token_copy(0).wait()
        wait(0)
        gate_pre = product(gate, held[:, :width])
        wait(1)
        up_pre = product(up, held[:, :width])
        if third == 0:
            token_copy(1).wait()
            lane = lax.broadcasted_iota(jnp.int32, (8, LANES), 1)
            expert = route_ref[4]
            chosen = ((lane == expert) | (lane == expert + LANES // 2)).astype(F32).astype(BF16)
            prob = lax.dot_general(
                chosen, held[:, 2 * width :], by_features, preferred_element_type=F32
            )[0:1]
        wait(2)
        hidden_grad = prob * product(down, held[:, width : 2 * width])
        sigmoid = jax.nn.sigmoid(gate_pre)
        active = gate_pre * sigmoid
        slope = sigmoid * (1.0 + gate_pre * (1.0 - sigmoid))
        stage[0, span] = (hidden_grad * up_pre * slope).astype(BF16)
        stage[1, span] = (hidden_grad * active).astype(BF16)
        stage[2, span] = (prob * active * up_pre).astype(BF16)
        for place in range(owners):
            if third * block < (place + 1) * share <= (third + 1) * block:
                for copy in flush(place):
                    copy.start()
    for place in range(owners):
        for copy in flush(place):
            copy.wait()


def hidden_rows(gathered, start, rows, route, w_gate, w_up, w_down):
    owners, share, width = w_gate.shape
    whole = pl.BlockSpec(memory_space=pl.ANY)
    kept = pltpu.VMEM((owners * share, width), BF16)
    return pl.pallas_call(
        functools.partial(hidden_kernel, start),
        grid_spec=pltpu.PrefetchScalarGridSpec(
            num_scalar_prefetch=1,
            grid=(1,),
            in_specs=[whole, whole, whole, whole],
            out_specs=[whole, whole, whole],
            scratch_shapes=[
                pltpu.VMEM((rows, gathered.shape[1]), BF16),
                kept,
                kept,
                kept,
                pltpu.VMEM((3, owners * share, rows), BF16),
                pltpu.SemaphoreType.DMA((2,)),
                pltpu.SemaphoreType.DMA((3, owners)),
                pltpu.SemaphoreType.DMA((owners, 3)),
            ],
        ),
        out_shape=[
            jax.ShapeDtypeStruct((3, owners, share, rows), BF16),
            jax.ShapeDtypeStruct((3, 2, share, rows), BF16),
            jax.ShapeDtypeStruct((3, 2, share, rows), BF16),
        ],
        compiler_params=pltpu.CompilerParams(vmem_limit_bytes=VMEM_LIMIT),
        cost_estimate=SMALL,
        name="hidden_rows",
    )(route, gathered, w_gate, w_up, w_down)


def input_kernel(core_ref, hidden_ref, gate_ref, up_ref, kept_ref, *rest):
    given_refs, turned = rest[:-1], rest[-1]
    count = pl.num_programs(0) // len(given_refs)

    @pl.when(pl.program_id(0) == 0)
    def _():
        turned[0] = hidden_ref[0].T
        turned[1] = hidden_ref[1].T

    total = jnp.dot(turned[0], gate_ref[...], preferred_element_type=F32)
    total += jnp.dot(turned[1], up_ref[...], preferred_element_type=F32)
    groups, share, step = kept_ref.shape
    total = total.astype(BF16).reshape(groups, 2, share, step)

    mine = core_ref[0] == 0
    kept_ref[...] = jnp.where(mine, total[:, 0], total[:, 1])
    for index, given_ref in enumerate(given_refs):

        @pl.when(pl.program_id(0) // count == index)
        def _():
            given_ref[...] = jnp.where(mine, total[:, 1], total[:, 0])


def input_rows(hidden, core, w_gate, w_up, share):
    _, units, token_count = hidden.shape
    width = w_gate.shape[1]
    step = 512
    groups = token_count // (2 * share)
    weight = pl.BlockSpec((units, step), lambda i, c: (0, i))
    part = pl.BlockSpec((groups, share, step), lambda i, c: (0, 0, i))
    shape = jax.ShapeDtypeStruct((groups, share, width), BF16)
    given_shape = jax.ShapeDtypeStruct((groups, share, width // GIVEN), BF16)
    count = width // step // GIVEN

    def given_part(index):
        return pl.BlockSpec(
            (groups, share, step),
            lambda i, c: (0, 0, jnp.clip(i - index * count, 0, count - 1)),
        )

    return pl.pallas_call(
        input_kernel,
        grid_spec=pltpu.PrefetchScalarGridSpec(
            num_scalar_prefetch=1,
            grid=(width // step,),
            in_specs=[pl.BlockSpec((2, units, token_count), lambda i, c: (0, 0, 0)), weight, weight],
            out_specs=[part] + [given_part(index) for index in range(GIVEN)],
            scratch_shapes=[pltpu.VMEM((2, token_count, units), BF16)],
        ),
        out_shape=[shape] + [given_shape] * GIVEN,
        compiler_params=pltpu.CompilerParams(vmem_limit_bytes=VMEM_LIMIT),
        cost_estimate=SMALL,
        name="input_rows",
    )(core, hidden, w_gate, w_up)


def pair_kernel(kept_ref, *refs):
    parts, out_ref = refs[:-1], refs[-1]
    step = parts[0].shape[2]
    for index, part in enumerate(parts):
        span = slice(index * step, (index + 1) * step)
        out_ref[:, :, span] = (kept_ref[:, :, span].astype(F32) + part[...].astype(F32)).astype(BF16)


def pair_sum(kept, parts):
    groups, share, width = kept.shape
    count = 4
    whole = pl.BlockSpec((groups // count, share, width), lambda i: (i, 0, 0))
    part = pl.BlockSpec((groups // count, share, width // len(parts)), lambda i: (i, 0, 0))
    return pl.pallas_call(
        pair_kernel,
        grid=(count,),
        in_specs=[whole] + [part] * len(parts),
        out_specs=whole,
        out_shape=jax.ShapeDtypeStruct(kept.shape, BF16),
        compiler_params=pltpu.CompilerParams(vmem_limit_bytes=VMEM_LIMIT),
        cost_estimate=SMALL,
        name="pair_sum",
    )(kept, *parts)


def own_kernel(
    pick_ref, first_ref, second_ref, tokens_ref, grads_ref, gate_ref, up_ref, down_ref, left
):
    share = first_ref.shape[2]

    @pl.when(pl.program_id(1) == 0)
    def _():
        for which in range(3):
            left[2 * share * which : 2 * share * which + share] = first_ref[which, 0]
            left[2 * share * which + share : 2 * share * (which + 1)] = second_ref[which, 0]

    both = jnp.dot(left[: 4 * share], tokens_ref[...], preferred_element_type=F32)
    gate_ref[0] = both[: 2 * share].astype(BF16)
    up_ref[0] = both[2 * share :].astype(BF16)
    down_ref[0] = jnp.dot(
        left[4 * share :], grads_ref[...], preferred_element_type=F32
    ).astype(BF16)


def own_grads(picks, hidden, gathered, width):
    _, _, share, token_count = hidden.shape
    step = 512
    count = width // 2 // step
    out = pl.BlockSpec((1, 2 * share, step), lambda h, i, p: (h, 0, i))
    shape = jax.ShapeDtypeStruct((2, 2 * share, width // 2), BF16)
    return pl.pallas_call(
        own_kernel,
        grid_spec=pltpu.PrefetchScalarGridSpec(
            num_scalar_prefetch=1,
            grid=(2, count),
            in_specs=[
                pl.BlockSpec((3, 1, share, token_count), lambda h, i, p: (0, p[2 * h], 0, 0)),
                pl.BlockSpec((3, 1, share, token_count), lambda h, i, p: (0, p[2 * h + 1], 0, 0)),
                pl.BlockSpec((token_count, step), lambda h, i, p: (0, h * count + i)),
                pl.BlockSpec((token_count, step), lambda h, i, p: (0, (2 + h) * count + i)),
            ],
            out_specs=[out, out, out],
            scratch_shapes=[pltpu.VMEM((6 * share, token_count), BF16)],
        ),
        out_shape=[shape, shape, shape],
        compiler_params=pltpu.CompilerParams(vmem_limit_bytes=VMEM_LIMIT),
        cost_estimate=SMALL,
        name="own_grads",
    )(picks, hidden, hidden, gathered, gathered)


def weight_kernel(other_ref, near_ref, own_ref, out_first, out_second):
    share = out_first.shape[0]
    left = other_ref[0].reshape(2 * share, other_ref.shape[3])
    total = own_ref[0].astype(F32) + jnp.dot(left, near_ref[...], preferred_element_type=F32)
    out_first[...] = total[:share].astype(BF16)
    out_second[...] = total[share:].astype(BF16)


def weight_grads(which, half, other, gathered_near, own):
    _, _, share, token_count = other.shape
    columns = gathered_near.shape[1] // 4
    step = 1024
    count = columns // step
    near_base = (half * 2 + which // 2) * count
    out = pl.BlockSpec((share, step), lambda i: (0, i))
    shape = jax.ShapeDtypeStruct((share, columns), BF16)
    return pl.pallas_call(
        weight_kernel,
        grid=(count,),
        in_specs=[
            pl.BlockSpec((1, 2, share, token_count), lambda i: (which, 0, 0, 0)),
            pl.BlockSpec((token_count, step), lambda i: (0, near_base + i)),
            pl.BlockSpec((1, 2 * share, step), lambda i: (half, 0, i)),
        ],
        out_specs=[out, out],
        out_shape=[shape, shape],
        compiler_params=pltpu.CompilerParams(vmem_limit_bytes=VMEM_LIMIT),
        cost_estimate=SMALL,
        name="weight_grads",
    )(other, gathered_near, own)


def per_device(tokens, out_grad, expert_ids, gate_probs, w_gate, w_up, w_down):
    token_count, width = tokens.shape
    half = width // 2
    owners = lax.axis_size("dp")
    ranks = lax.axis_size(("xl", "core"))
    experts = lax.axis_size(PLANE)
    units = w_gate.shape[1]
    share = token_count // ranks
    rank = lax.axis_index(("xl", "core"))
    core = lax.axis_index("core")
    expert = lax.axis_index(PLANE)
    place = lax.axis_index("dp")
    side = place ^ 1
    mirror = owners - 1 - place
    to_side = [(i, i ^ 1) for i in range(owners)]
    to_mirror = [(i, owners - 1 - i) for i in range(owners)]

    def own_share(array):
        return lax.dynamic_slice_in_dim(array, rank * share, share, 0)

    my_tokens, my_grads = own_share(tokens), own_share(out_grad)
    hits = own_share(expert_ids)[:, :, None] == jnp.arange(experts, dtype=jnp.int32)
    table = jnp.sum(jnp.where(hits, own_share(gate_probs)[:, :, None], 0.0), axis=1)
    coarse = table.astype(BF16)
    fine = (table - coarse.astype(F32)).astype(BF16)
    pad = jnp.zeros((share, LANES // 2 - experts), BF16)
    payload = jnp.concatenate([my_tokens, my_grads, coarse, pad, fine, pad], axis=1)
    gathered = lax.all_gather(payload, PLANE, axis=0, tiled=True)
    from_side = lax.ppermute(
        jnp.concatenate([my_tokens[:, :half], my_grads[:, :half]], axis=1), "dp", to_side
    )
    from_mirror = lax.ppermute(
        jnp.concatenate([my_tokens[:, half:], my_grads[:, half:]], axis=1), "dp", to_mirror
    )
    near_payload = jnp.concatenate([from_side, from_mirror], axis=1)
    gathered, near_payload = lax.optimization_barrier((gathered, near_payload))
    gathered_near = lax.all_gather(near_payload, PLANE, axis=0, tiled=True)

    route = jnp.stack([side, place ^ 2, mirror, place, expert]).astype(jnp.int32)
    gate, up, down = (w.reshape(owners, units // owners, width) for w in (w_gate, w_up, w_down))
    hidden, for_side, for_mirror = hidden_rows(
        gathered, 0, gathered.shape[0], route, gate, up, down
    )
    other_side = lax.ppermute(for_side, "dp", to_side)
    other_mirror = lax.ppermute(for_mirror, "dp", to_mirror)

    kept, *given = input_rows(
        hidden.reshape(3, units, -1), core[None], w_gate[0], w_up[0], share
    )
    picks = jnp.stack([place, mirror, side, place]).astype(jnp.int32)
    own = own_grads(picks, hidden, gathered, width)
    taken = [lax.ppermute(part, "core", [(0, 1), (1, 0)]) for part in given]
    paired = pair_sum(kept, taken)
    paired, own, other_side, other_mirror = lax.optimization_barrier(
        (paired, own, other_side, other_mirror)
    )
    returned = lax.all_to_all(paired, PLANE[:3], split_axis=0, concat_axis=0, tiled=True)

    mine, theirs = [], []
    for which in (2, 0, 1):
        mine_low, theirs_low = weight_grads(which, 0, other_side, gathered_near, own[which])
        theirs_high, mine_high = weight_grads(which, 1, other_mirror, gathered_near, own[which])
        mine.append((mine_low, mine_high))
        theirs.append((theirs_low, theirs_high))
    received = [
        (lax.ppermute(low, "dp", to_mirror), lax.ppermute(high, "dp", to_side)) for low, high in theirs
    ]
    results = []
    for (mine_low, mine_high), (low, high) in zip(mine, received):
        if len(results) == 2:
            returned, low, high, results = lax.optimization_barrier((returned, low, high, results))
        low = mine_low.astype(F32) + low.astype(F32)
        high = mine_high.astype(F32) + high.astype(F32)
        results.append(jnp.concatenate([low, high], axis=1).astype(BF16)[None])
    in_grad = jnp.sum(returned.astype(F32), axis=0).astype(BF16)
    return (in_grad, results[1], results[2], results[0])


def solution(mesh):
    dp, ctx, tensor = (mesh.shape[name] for name in ("dp", "ctx", "tensor"))
    fine = Mesh(
        mesh.devices.reshape(dp, ctx // 2, 2, tensor // 2, 2), ("dp", "z", "xh", "xl", "core")
    )
    token_spec = P(("dp", "z", "xh"), None)
    weight_spec = P(PLANE, None, None)
    grad_spec = P(PLANE, "dp", None)
    return jax.shard_map(
        per_device,
        mesh=fine,
        in_specs=(token_spec,) * 4 + (weight_spec,) * 3,
        out_specs=(P(("dp",) + PLANE, None), grad_spec, grad_spec, grad_spec),
        check_vma=False,
    )
```
